256 devices in a mesh: dom: 32 (over y, z), feat: 8 (over x, core).
Axes of the slice: x: 4, y: 4, z: 8, core: 2. Of those that a mesh axis runs over, the one named last changes fastest.
Arguments:
- feats: bfloat16 [128, 262144], P('feat', 'dom'), may hold values from -6 to 6
- tile_vals: bfloat16 [10240, 128, 128], P('dom'), may hold values from -0.1875 to 0.1875
- tile_dst: int32 [10240], P('dom'), may hold values from 0 to 63
- tile_src: int32 [10240], P('dom'), may hold values from 0 to 111
- tile_count: int32 [32], P('dom'), may hold values from 80 to 320, as said below
- send_rows: int32 [32, 32, 64], P('dom'), may hold values from 0 to 8191
- hub_ids: int32 [4096], P('dom'), may hold values from 0 to 8191, as said below
- w_self: bfloat16 [128, 128], P('feat'), may hold values from -0.5 to 0.5
- w_neigh: bfloat16 [128, 128], P('feat'), may hold values from -0.5 to 0.5
- bias: float32 [128], P('feat'), may hold values from -3 to 3
- cotangent: bfloat16 [128, 262144], P('feat', 'dom'), may hold values from -6 to 6
Outputs:
- activated: bfloat16 [128, 262144], P('feat', 'dom')
- grad_feats: bfloat16 [128, 262144], P('feat', 'dom')
- grad_w_self: float32 [128, 128], P('feat')
- grad_w_neigh: float32 [128, 128], P('feat')
- grad_bias: float32 [128], P('feat')
The draws below stay inside these ranges and needn't reach their ends.
Inputs may be any that keep to these rules, and one draw needn't show every extreme that they name: `tile_count`: the live tiles of a partition are its first ones; some partition has all 320 slots live. `hub_ids`: the 128 entries of one partition are distinct rows of that partition.
All inputs are finite; a program needn't handle non-finite values.
Results may differ from the reference program's by a relative error of at most 0.0075.
Values may be sent and summed in bfloat16 or wider, within the bound.
No kernel may reach another device: no remote copies, remote signals or barrier semaphores. Data moves between devices by JAX's collectives and lax.ppermute only.
A program may use at most 64 MiB of HBM per device.

```python
import math
import jax
import jax.numpy as jnp
from jax import lax

F = 128
NODE_DEV = 8192
SLOT = 64
HUB_DEV = 128
TILE_DEV = 320
NODES = 262144
TILES = 10240
EXT_BLK = 112
N_DOM = 32


def draw_tile_count(key, part):
    key = jax.random.fold_in(key, 11)
    extent = 3 * TILE_DEV // 4 + 1
    drawn_values = jax.random.randint(key, (3, N_DOM), 0, extent)
    surplus = drawn_values[0] * drawn_values[1] // extent * drawn_values[2] // extent
    counts = TILE_DEV // 4 + surplus
    heaviest = jax.random.randint(jax.random.fold_in(key, 5), (), 0, N_DOM)
    return jnp.where(jnp.arange(N_DOM) == heaviest, TILE_DEV, counts).astype(jnp.int32)


def first_rows(subkey):
    return jax.random.permutation(subkey, NODE_DEV)[:HUB_DEV]


def draw_hub_ids(key, part):
    key = jax.random.fold_in(key, 23)
    subkeys = jax.random.split(key, N_DOM)
    hub_rows = jax.vmap(first_rows)(subkeys)
    return hub_rows.reshape(-1).astype(jnp.int32)


def set_ends(drawn, rng, least, largest):
    dims = drawn.shape
    place = [jax.random.randint(jax.random.fold_in(rng, axis), (), 0, dims[axis]) for axis in range(len(dims))]
    drawn = drawn.at[tuple(place)].set(least)
    longest = dims.index(max(dims))
    place[longest] = (place[longest] + 1) % dims[longest]
    return drawn.at[tuple(place)].set(largest)


def block_scale(stream_key, shape, cuts, least, top_value):
    gain, own = 1.0, jax.random.fold_in(stream_key, 6)
    for dim, blocks in cuts:
        steps = jnp.exp(jax.random.uniform(jax.random.fold_in(own, dim), (blocks,), jnp.float32, least / len(cuts), top_value / len(cuts)))
        gain = gain * jnp.repeat(steps, shape[dim] // blocks).reshape([-1 if axis == dim else 1 for axis in range(len(shape))])
    return gain


def gaussian(rng, shape, scale, reach, cuts=(), kind=jnp.bfloat16):
    drawn = jax.random.normal(rng, shape, jnp.float32) * scale
    if len(cuts) > 0:
        drawn = block_scale(rng, shape, cuts, -0.22, 0.18) * drawn
    return jnp.clip(drawn, min=-reach, max=reach).astype(kind)


def setup_inputs(seed: int = 0) -> dict:
    seeds = jax.random.split(jax.random.key(seed), 12)
    feats = gaussian(seeds[0], (F, NODES), 1.0, 6.0, ((0, 8), (1, 32)))
    tile_vals = gaussian(seeds[1], (TILES, 128, 128), 1024 ** -0.5, 0.1875, ((0, 32),))
    tile_dst = set_ends(jax.random.randint(seeds[2], (TILES,), 0, NODE_DEV // 128), jax.random.fold_in(seeds[2], 1), 0, (NODE_DEV // 128) - 1).astype(jnp.int32)
    tile_src = set_ends(jax.random.randint(seeds[3], (TILES,), 0, EXT_BLK), jax.random.fold_in(seeds[3], 1), 0, EXT_BLK - 1).astype(jnp.int32)
    tile_count = draw_tile_count(jax.random.fold_in(seeds[11], 71), 0)
    send_rows = set_ends(jax.random.randint(seeds[5], (N_DOM, N_DOM, SLOT), 0, NODE_DEV), jax.random.fold_in(seeds[5], 1), 0, NODE_DEV - 1).astype(jnp.int32)
    hub_ids = draw_hub_ids(jax.random.fold_in(seeds[11], 71), 0)
    w_self = gaussian(seeds[7], (F, F), F ** -0.5, 0.5, ((0, 8),))
    w_neigh = gaussian(seeds[8], (F, F), F ** -0.5, 0.5, ((0, 8),))
    bias = gaussian(seeds[9], (F,), 0.5, 3.0, ((0, 8),), jnp.float32)
    cotangent = gaussian(seeds[10], (F, NODES), 1.0, 6.0, ((0, 8), (1, 32)))
    return dict(feats=feats, tile_vals=tile_vals, tile_dst=tile_dst, tile_src=tile_src, tile_count=tile_count, send_rows=send_rows, hub_ids=hub_ids, w_self=w_self, w_neigh=w_neigh, bias=bias, cotangent=cotangent)


def silu_slope(values):
    logistic = jax.nn.sigmoid(values)
    return logistic * (1.0 + values * (1.0 - logistic))

def reference(feats, tile_vals, tile_dst, tile_src, tile_count, send_rows, hub_ids, w_self, w_neigh, bias, cotangent):
    node_blocks = NODE_DEV // 128
    recv_rows = N_DOM * SLOT
    ext_rows = NODE_DEV + recv_rows + HUB_DEV * N_DOM
    ext_blocks = ext_rows // 128
    offsets = jnp.arange(N_DOM, dtype=jnp.int32) * NODE_DEV
    hub_global = (hub_ids.reshape(N_DOM, HUB_DEV) + offsets[:, None]).reshape(-1).astype(jnp.int32)
    send_global = (send_rows + offsets[:, None, None]).astype(jnp.int32)
    hub_table = jnp.take(feats, hub_global, axis=1)
    tiles_all = tile_vals.reshape(N_DOM, TILE_DEV, 128, 128)
    targets_all = tile_dst.reshape(N_DOM, TILE_DEV)
    sources_all = tile_src.reshape(N_DOM, TILE_DEV)
    live_all = (jnp.arange(TILE_DEV, dtype=jnp.int32)[None, :] < tile_count[:, None]).astype(jnp.float32)
    owners = jnp.arange(N_DOM, dtype=jnp.int32)

    def aggregate_one(owner):
        own_rows = lax.dynamic_slice_in_dim(feats, owner * NODE_DEV, NODE_DEV, 1)
        incoming = jnp.take(feats, send_global[:, owner, :].reshape(-1), axis=1)
        extended = jnp.concatenate([own_rows, incoming, hub_table], axis=1)
        blocks = extended.reshape(F, ext_blocks, 128).transpose(1, 0, 2).astype(jnp.float32)
        picked = blocks[sources_all[owner]]
        products = jnp.einsum('gfs,gds->gfd', picked, tiles_all[owner].astype(jnp.float32))
        products = products * live_all[owner][:, None, None]
        summed = jnp.zeros((node_blocks, F, 128), jnp.float32).at[targets_all[owner]].add(products)
        return summed.transpose(1, 0, 2).reshape(F, NODE_DEV).astype(jnp.bfloat16)
    aggregate = lax.map(aggregate_one, owners)
    aggregate = aggregate.transpose(1, 0, 2).reshape(F, N_DOM * NODE_DEV)
    linear = jnp.dot(w_self.T, feats, preferred_element_type=jnp.float32)
    linear = linear + jnp.dot(w_neigh.T, aggregate, preferred_element_type=jnp.float32)
    linear = linear + bias[:, None]
    activated = jax.nn.silu(linear).astype(jnp.bfloat16)
    grad_linear = (cotangent.astype(jnp.float32) * silu_slope(linear)).astype(jnp.bfloat16)
    scale = 1.0 / math.sqrt(N_DOM * NODE_DEV)
    grad_w_self = jnp.dot(feats, grad_linear.T, preferred_element_type=jnp.float32) * scale
    grad_w_neigh = jnp.dot(aggregate, grad_linear.T, preferred_element_type=jnp.float32) * scale
    grad_bias = lax.optimization_barrier(jnp.sum(grad_linear.astype(jnp.float32), axis=1)) * scale
    grad_aggregate = jnp.dot(w_neigh, grad_linear, preferred_element_type=jnp.float32).astype(jnp.bfloat16)
    grad_feats = jnp.dot(w_self, grad_linear, preferred_element_type=jnp.float32)

    def spread_one(owner):
        own_rows = lax.dynamic_slice_in_dim(grad_aggregate, owner * NODE_DEV, NODE_DEV, 1)
        blocks = own_rows.reshape(F, node_blocks, 128).transpose(1, 0, 2).astype(jnp.float32)
        picked = blocks[targets_all[owner]]
        products = jnp.einsum('gfd,gds->gfs', picked, tiles_all[owner].astype(jnp.float32))
        products = products * live_all[owner][:, None, None]
        summed = jnp.zeros((ext_blocks, F, 128), jnp.float32).at[sources_all[owner]].add(products)
        return summed.transpose(1, 0, 2).reshape(F, ext_rows)
    spread = lax.map(spread_one, owners)
    own_part = spread[:, :, :NODE_DEV].transpose(1, 0, 2).reshape(F, N_DOM * NODE_DEV)
    grad_feats = grad_feats + own_part
    remote = spread[:, :, NODE_DEV:NODE_DEV + recv_rows].astype(jnp.bfloat16)
    remote = lax.optimization_barrier(remote).astype(jnp.float32)
    remote = remote.reshape(N_DOM, F, N_DOM, SLOT).transpose(1, 2, 0, 3).reshape(F, N_DOM * N_DOM * SLOT)
    grad_feats = grad_feats.at[:, send_global.reshape(-1)].add(remote)
    hub_part = lax.optimization_barrier(jnp.sum(spread[:, :, NODE_DEV + recv_rows:], axis=0))
    grad_feats = grad_feats.at[:, hub_global].add(hub_part)
    return (activated, grad_feats.astype(jnp.bfloat16), grad_w_self, grad_w_neigh, grad_bias)
```

```python
import functools
import math

import jax
import jax.numpy as jnp
from jax import lax
from jax.experimental import pallas as pl
from jax.experimental.pallas import tpu as pltpu
from jax.sharding import PartitionSpec as P

edge = 128
group = 8
chunk = 32
bf16 = jnp.bfloat16
f32 = jnp.float32
vmem = pl.BlockSpec(memory_space=pltpu.VMEM)
smem = pl.BlockSpec(memory_space=pltpu.SMEM)
hbm = pl.BlockSpec(memory_space=pl.ANY)


def params():
    return pltpu.CompilerParams(vmem_limit_bytes=48 * 1024 * 1024)


def lanes(rows):
    return lax.broadcasted_iota(jnp.int32, (rows, edge), 1)


def split(values, pieces):
    parts = []
    for _ in range(pieces):
        part = values.astype(bf16)
        parts.append(part)
        values = values - part.astype(f32)
    return parts


def column_block(column):
    hi, mid, lo = split(column, 3)
    lane = lanes(column.shape[0])
    block = jnp.where(lane == 0, hi.astype(f32), 0.0)
    block = jnp.where(lane == 1, mid.astype(f32), block)
    return jnp.where(lane == 2, lo.astype(f32), block)


def pick_kernel(index_ref, feats_ref, out_ref, blocks, picked):
    width, nodes = feats_ref.shape
    count = nodes // edge
    for b in range(count):
        blocks[b] = feats_ref[:, b * edge : (b + 1) * edge]
    whole = blocks[...].reshape(count * width, edge)
    sub = lax.broadcasted_iota(jnp.int32, (edge, edge), 0)

    def step(g, carry):
        index = index_ref[pl.ds(g, 1), :]
        place = index & (edge - 1)
        home = index >> 7
        hot = jnp.where(sub == place, 1.0, 0.0).astype(bf16)
        found = jnp.dot(whole, hot, preferred_element_type=f32)
        home = jnp.broadcast_to(home, (width, edge))
        total = jnp.zeros((width, edge), f32)
        for b in range(count):
            total = jnp.where(home == b, found[b * width : (b + 1) * width], total)
        picked[g] = total
        return carry

    groups = picked.shape[0]
    lax.fori_loop(0, groups, step, 0)
    lane = lanes(width)
    hub = picked[groups - 1].astype(bf16)
    for g in range(groups - 1):
        here = picked[g]
        turned = pltpu.roll(here, edge // 2, 1)
        for odd in range(2):
            first, second = (turned, here) if odd else (here, turned)
            out_ref[2 * g + odd, 0:width] = hub
            out_ref[2 * g + odd, width : 2 * width] = jnp.where(
                lane < edge // 2, first, second
            ).astype(bf16)


def pick(index, feats, domains):
    width, nodes = feats.shape
    groups = domains // 2 + 1
    return pl.pallas_call(
        pick_kernel,
        out_shape=jax.ShapeDtypeStruct((domains, 2 * width, edge), bf16),
        in_specs=[vmem, vmem],
        out_specs=vmem,
        scratch_shapes=[
            pltpu.VMEM((nodes // edge, width, edge), bf16),
            pltpu.VMEM((groups, width, edge), f32),
        ],
        compiler_params=params(),
        name="pick",
    )(index, feats)


def deal_kernel(feats_ref, cotangent_ref, self_ref, neigh_ref, bias_ref, out_ref):
    width, nodes = feats_ref.shape
    peers = out_ref.shape[0]
    share = nodes // peers
    bias = column_block(bias_ref[...]).astype(bf16)
    for k in range(peers):
        out_ref[k, :, 0:share] = feats_ref[:, k * share : (k + 1) * share]
        out_ref[k, :, share : 2 * share] = cotangent_ref[:, k * share : (k + 1) * share]
        out_ref[k, :, 2 * share : 2 * share + edge] = self_ref[...]
        out_ref[k, :, 2 * share + edge : 2 * share + 2 * edge] = neigh_ref[...]
        out_ref[k, :, 2 * share + 2 * edge : 2 * share + 3 * edge] = bias


def deal(feats, cotangent, w_self, w_neigh, bias, peers):
    width, nodes = feats.shape
    return pl.pallas_call(
        deal_kernel,
        out_shape=jax.ShapeDtypeStruct((peers, width, 2 * nodes // peers + 3 * edge), bf16),
        in_specs=[vmem] * 5,
        out_specs=vmem,
        compiler_params=params(),
        name="deal",
    )(feats, cotangent, w_self, w_neigh, bias[:, None])


def tile_walk(vals_ref, held, sems, count, visit):
    total = vals_ref.shape[0]
    chunks = total // chunk

    def copy(c):
        rows = pl.ds(c * chunk, chunk)
        return pltpu.make_async_copy(vals_ref.at[rows], held.at[rows], sems.at[c])

    live_chunks = (count + chunk - 1) // chunk

    def begin(c, carry):
        copy(c).start()
        return carry

    def finish(c, carry):
        copy(c).wait()
        first = c * chunk
        steps = (jnp.minimum(count - first, chunk) + group - 1) // group

        def some(i, inner):
            visit(first + i * group)
            return inner

        lax.fori_loop(0, steps, some, 0)
        return carry

    lax.fori_loop(0, live_chunks, begin, 0)
    return lambda: lax.fori_loop(0, live_chunks, finish, 0)


def gather_kernel(
    dst_ref, src_ref, count_ref, feats_ref, recv_ref, vals_ref, out_ref, ext, total, held, sems
):
    width, nodes = feats_ref.shape
    own = nodes // edge
    domains = recv_ref.shape[0]
    count = count_ref[0]

    def visit(first):
        products = []
        places = []
        for i in range(group):
            t = first + i
            products.append(
                lax.dot_general(
                    ext[src_ref[t]],
                    held[t],
                    (((1,), (1,)), ((), ())),
                    preferred_element_type=f32,
                )
            )
            places.append(jnp.where(t < count, dst_ref[t], own))
        for place, product in zip(places, products):
            total[place] += product

    walk = tile_walk(vals_ref, held, sems, count, visit)
    lane = lanes(width)
    for b in range(own):
        ext[b] = feats_ref[:, b * edge : (b + 1) * edge]
    for g in range(domains // 2):
        ext[own + g] = jnp.where(
            lane < edge // 2,
            recv_ref[2 * g, width : 2 * width].astype(f32),
            recv_ref[2 * g + 1, width : 2 * width].astype(f32),
        ).astype(bf16)
    for q in range(domains):
        ext[own + domains // 2 + q] = recv_ref[q, 0:width]
    total[...] = jnp.zeros_like(total)
    walk()
    peers = out_ref.shape[0]
    per = own // peers
    for b in range(own):
        col = (b % per) * edge
        out_ref[b // per, :, col : col + edge] = total[b].astype(bf16)


def gather(dst, src, count, feats, recv, vals, peers):
    width, nodes = feats.shape
    domains = recv.shape[0]
    own = nodes // edge
    tiles = vals.shape[0]
    return pl.pallas_call(
        gather_kernel,
        out_shape=jax.ShapeDtypeStruct((peers, width, nodes // peers), bf16),
        in_specs=[smem, smem, smem, vmem, vmem, hbm],
        out_specs=vmem,
        scratch_shapes=[
            pltpu.VMEM((own + domains // 2 + domains, width, edge), bf16),
            pltpu.VMEM((own + 1, width, edge), f32),
            pltpu.VMEM((tiles, edge, edge), bf16),
            pltpu.SemaphoreType.DMA((tiles // chunk,)),
        ],
        compiler_params=params(),
        name="gather",
    )(dst, src, count, feats, recv, vals)


def spread_kernel(
    dst_ref, src_ref, count_ref, grads_ref, vals_ref, out_ref, own_ref, blocks, total, held, sems
):
    peers, width, _ = grads_ref.shape
    own = own_ref.shape[0]
    per = own // peers
    share = per * edge
    domains = out_ref.shape[0]
    far = own + domains // 2
    spare = far + domains
    count = count_ref[0]

    def visit(first):
        products = []
        places = []
        for i in range(group):
            t = first + i
            products.append(
                jnp.dot(blocks[dst_ref[t]], held[t], preferred_element_type=f32)
            )
            places.append(jnp.where(t < count, src_ref[t], spare))
        for place, product in zip(places, products):
            total[place] += product

    walk = tile_walk(vals_ref, held, sems, count, visit)
    for b in range(own):
        col = (b % per) * edge
        blocks[b] = grads_ref[b // per, :, col : col + edge]
    total[...] = jnp.zeros_like(total)

    def summed(place):
        return jnp.sum(grads_ref[:, :, share + place * edge : share + (place + 1) * edge].astype(f32), axis=0)

    grad_self = (summed(0) + summed(1)).astype(bf16)
    grad_neigh = (summed(2) + summed(3)).astype(bf16)
    grad_bias = column_block(jnp.sum(summed(4), axis=1, keepdims=True))
    walk()
    own_ref[...] = total[0:own]
    lane = lanes(width)
    grad_bias = pltpu.roll(grad_bias, edge // 2, 1)
    for g in range(domains // 2):
        here = total[own + g]
        for odd in range(2):
            q = 2 * g + odd
            mine = pltpu.roll(here, edge // 2, 1) if odd else here
            out_ref[q, 0:width] = total[far + q].astype(bf16)
            out_ref[q, width : 2 * width] = jnp.where(lane < edge // 2, mine, grad_bias).astype(bf16)
            out_ref[q, 2 * width : 3 * width] = grad_self
            out_ref[q, 3 * width : 4 * width] = grad_neigh


def spread(dst, src, count, grads, vals, domains, nodes):
    _, width, _ = grads.shape
    own = nodes // edge
    tiles = vals.shape[0]
    return pl.pallas_call(
        spread_kernel,
        out_shape=(
            jax.ShapeDtypeStruct((domains, 4 * width, edge), bf16),
            jax.ShapeDtypeStruct((own, width, edge), f32),
        ),
        in_specs=[smem, smem, smem, vmem, hbm],
        out_specs=(vmem, vmem),
        scratch_shapes=[
            pltpu.VMEM((own, width, edge), bf16),
            pltpu.VMEM((own + domains // 2 + domains + 1, width, edge), f32),
            pltpu.VMEM((tiles, edge, edge), bf16),
            pltpu.SemaphoreType.DMA((tiles // chunk,)),
        ],
        compiler_params=params(),
        name="spread",
    )(dst, src, count, grads, vals)


def layer_kernel(dealt_ref, agg_ref, near_ref, late_ref):
    peers, width, share = agg_ref.shape
    rows = peers * width

    def part(start, size):
        return dealt_ref[:, :, start : start + size].reshape(rows, size)

    feats = part(0, share)
    cotangent = part(share, share)
    w_self = part(2 * share, edge)
    w_neigh = part(2 * share + edge, edge)
    bias = jnp.sum(part(2 * share + 2 * edge, edge).astype(f32), axis=1, keepdims=True)
    aggregate = agg_ref[...].reshape(rows, share)
    first = (((0,), (0,)), ((), ()))
    last = (((1,), (1,)), ((), ()))
    linear = lax.dot_general(w_self, feats, first, preferred_element_type=f32)
    linear = linear + lax.dot_general(w_neigh, aggregate, first, preferred_element_type=f32)
    linear = linear + bias
    logistic = jax.nn.sigmoid(linear)
    late_ref[:, :, 0:share] = (linear * logistic).astype(bf16).reshape(peers, width, share)
    slope = logistic * (1.0 + linear * (1.0 - logistic))
    grad = (cotangent.astype(f32) * slope).astype(bf16)
    near_ref[:, :, 0:share] = (
        jnp.dot(w_neigh, grad, preferred_element_type=f32).astype(bf16).reshape(peers, width, share)
    )
    late_ref[:, :, share : 2 * share] = (
        jnp.dot(w_self, grad, preferred_element_type=f32).astype(bf16).reshape(peers, width, share)
    )
    grad_self = lax.dot_general(feats, grad, last, preferred_element_type=f32)
    grad_neigh = lax.dot_general(aggregate, grad, last, preferred_element_type=f32)
    grad_bias = column_block(jnp.sum(grad.astype(f32), axis=1, keepdims=True)).astype(bf16)
    pieces = split(grad_self, 2) + split(grad_neigh, 2) + [grad_bias]
    for place, piece in enumerate(pieces):
        near_ref[:, :, share + place * edge : share + (place + 1) * edge] = piece.reshape(
            peers, width, edge
        )


def layer(dealt, agg):
    peers, width, share = agg.shape
    return pl.pallas_call(
        layer_kernel,
        out_shape=(
            jax.ShapeDtypeStruct((peers, width, share + 5 * edge), bf16),
            jax.ShapeDtypeStruct((peers, width, 2 * share), bf16),
        ),
        in_specs=[vmem, vmem],
        out_specs=(vmem, vmem),
        compiler_params=params(),
        name="layer",
    )(dealt, agg)


def settle_kernel(
    scale,
    index_ref,
    recv_ref,
    late_ref,
    own_ref,
    act_ref,
    feats_ref,
    self_ref,
    neigh_ref,
    bias_ref,
    values,
    marked,
    placed,
):
    domains = recv_ref.shape[0]
    peers, width, share = late_ref.shape
    share = share // 2
    own = own_ref.shape[0]
    per = own // peers
    pairs = domains // 2
    lane = lanes(width)

    def over(start):
        return jnp.sum(recv_ref[:, start : start + width].astype(f32), axis=0)

    hub = over(0)
    self_ref[...] = over(2 * width) * scale
    neigh_ref[...] = over(3 * width) * scale
    tail = jnp.where(lane >= edge // 2, over(width), 0.0)
    bias_ref[...] = jnp.sum(tail, axis=1, keepdims=True) * scale
    for g in range(pairs):
        here = recv_ref[2 * g, width : 2 * width].astype(f32)
        other = pltpu.roll(recv_ref[2 * g + 1, width : 2 * width].astype(f32), edge // 2, 1)
        values[g] = jnp.where(lane < edge // 2, here, other)
    for k, piece in enumerate(split(hub, 3)):
        values[pairs + k] = piece.astype(f32)
    sub = lax.broadcasted_iota(jnp.int32, (edge, edge), 0)
    placed[...] = jnp.zeros_like(placed)

    def step(g, carry):
        index = index_ref[pl.ds(jnp.minimum(g, pairs), 1), :]
        place = index & (edge - 1)
        home = jnp.broadcast_to(index >> 7, (width, edge))
        hot = jnp.where(sub == place, 1.0, 0.0).astype(bf16)
        value = values[g]
        for b in range(own):
            marked[b] = jnp.where(home == b, value, 0.0).astype(bf16)
        placed[...] += lax.dot_general(
            marked[...].reshape(own * width, edge),
            hot,
            (((1,), (1,)), ((), ())),
            preferred_element_type=f32,
        )
        return carry

    lax.fori_loop(0, pairs + 3, step, 0)
    for k in range(peers):
        act_ref[:, k * share : (k + 1) * share] = late_ref[k, :, 0:share]
    for b in range(own):
        col = share + (b % per) * edge
        feats_ref[:, b * edge : (b + 1) * edge] = (
            late_ref[b // per, :, col : col + edge].astype(f32)
            + own_ref[b]
            + placed[b * width : (b + 1) * width]
        ).astype(bf16)


def settle(index, recv, late, own, scale):
    peers, width, share = late.shape
    nodes = own.shape[0] * edge
    domains = recv.shape[0]
    return pl.pallas_call(
        functools.partial(settle_kernel, scale),
        out_shape=(
            jax.ShapeDtypeStruct((width, nodes), bf16),
            jax.ShapeDtypeStruct((width, nodes), bf16),
            jax.ShapeDtypeStruct((width, edge), f32),
            jax.ShapeDtypeStruct((width, edge), f32),
            jax.ShapeDtypeStruct((width, 1), f32),
        ),
        in_specs=[vmem] * 4,
        out_specs=(vmem,) * 5,
        scratch_shapes=[
            pltpu.VMEM((domains // 2 + 3, width, edge), f32),
            pltpu.VMEM((own.shape[0], width, edge), bf16),
            pltpu.VMEM((own.shape[0] * width, edge), f32),
        ],
        compiler_params=params(),
        name="settle",
    )(index, recv, late, own)


def swap(values, axis):
    return lax.all_to_all(values, axis, split_axis=0, concat_axis=0, tiled=True)


def local(
    feats,
    tile_vals,
    tile_dst,
    tile_src,
    tile_count,
    send_rows,
    hub_ids,
    w_self,
    w_neigh,
    bias,
    cotangent,
):
    nodes = feats.shape[1]
    domains = lax.axis_size("dom")
    peers = lax.axis_size("feat")
    index = jnp.concatenate([send_rows.reshape(domains // 2, edge), hub_ids.reshape(1, edge)])
    recv = swap(pick(index, feats, domains), "dom")
    dealt = swap(deal(feats, cotangent, w_self, w_neigh, bias, peers), "feat")
    agg = swap(gather(tile_dst, tile_src, tile_count, feats, recv, tile_vals, peers), "feat")
    near, late = layer(dealt, agg)
    near = swap(near, "feat")
    late = swap(late, "feat")
    back, own = spread(tile_dst, tile_src, tile_count, near, tile_vals, domains, nodes)
    back = swap(back, "dom")
    scale = 1.0 / math.sqrt(nodes * domains)
    act, grad_feats, grad_self, grad_neigh, grad_bias = settle(index, back, late, own, scale)
    return act, grad_feats, grad_self, grad_neigh, grad_bias[:, 0]


def solution(mesh):
    placed = (
        P("feat", "dom"),
        P("dom", None, None),
        P("dom"),
        P("dom"),
        P("dom"),
        P("dom", None, None),
        P("dom"),
        P("feat", None),
        P("feat", None),
        P("feat"),
        P("feat", "dom"),
    )
    return jax.shard_map(
        local,
        mesh=mesh,
        in_specs=placed,
        out_specs=(P("feat", "dom"), P("feat", "dom"), P("feat", None), P("feat", None), P("feat")),
        check_vma=False,
    )
```

```python
import functools
import math

import jax
import jax.numpy as jnp
from jax import lax
from jax.experimental import pallas as pl
from jax.experimental.pallas import tpu as pltpu
from jax.sharding import PartitionSpec as P

edge = 128
span = 256
group = 32
bf16 = jnp.bfloat16
f32 = jnp.float32
vmem = pl.BlockSpec(memory_space=pltpu.VMEM)
smem = pl.BlockSpec(memory_space=pltpu.SMEM)
hbm = pl.BlockSpec(memory_space=pl.ANY)


def params(mib):
    return pltpu.CompilerParams(vmem_limit_bytes=mib * 1024 * 1024)


def far_off(*values):
    return [pltpu.with_memory_space_constraint(value, pltpu.HBM) for value in values]


def lanes(rows):
    return lax.broadcasted_iota(jnp.int32, (rows, edge), 1)


def split(values, pieces):
    parts = []
    for _ in range(pieces):
        part = values.astype(bf16)
        parts.append(part)
        values = values - part.astype(f32)
    return parts


def column_block(column):
    hi, mid, lo = split(column, 3)
    lane = lanes(column.shape[0])
    block = jnp.where(lane == 0, hi.astype(f32), 0.0)
    block = jnp.where(lane == 1, mid.astype(f32), block)
    return jnp.where(lane == 2, lo.astype(f32), block)


def pick_kernel(
    rows_ref, hub_ref, feats_ref, out_ref, hot_ref, home_ref, near, hub, wide, index, blocks, picked, sems
):
    width, nodes = feats_ref.shape
    count = nodes // span
    pairs = rows_ref.shape[0] // 2
    half = edge // 2
    copies = [
        pltpu.make_async_copy(feats_ref, near, sems.at[0]),
        pltpu.make_async_copy(rows_ref, wide, sems.at[1]),
        pltpu.make_async_copy(hub_ref, hub, sems.at[2]),
    ]
    for copy in copies:
        copy.start()
    copies[1].wait()
    copies[2].wait()
    lane = lanes(1)
    for g in range(pairs):
        row = jnp.concatenate([wide[2 * g : 2 * g + 1, :], wide[2 * g + 1 : 2 * g + 2, :]], axis=1)
        index[g : g + 1, :] = row
    index[pairs : pairs + 1, :] = hub[...].reshape(1, edge)
    home_ref[...] = index[...] >> 8
    copies[0].wait()
    for b in range(count):
        blocks[b] = near[:, b * span : (b + 1) * span]
    sub = lax.broadcasted_iota(jnp.int32, (span, edge), 0)

    def step(g, carry):
        place = index[pl.ds(g, 1), :] & (span - 1)
        home = jnp.broadcast_to(home_ref[pl.ds(g, 1), :], (width, edge))
        hot = jnp.where(sub == place, 1.0, 0.0).astype(bf16)
        hot_ref[g] = hot
        found = jnp.dot(blocks[...].reshape(count * width, span), hot, preferred_element_type=f32)
        total = found[0:width]
        for b in range(1, count):
            total = jnp.where(home == b, found[b * width : (b + 1) * width], total)
        picked[g] = total
        return carry

    lax.fori_loop(0, pairs, step, 0, unroll=4)
    step(pairs, 0)
    lane = lanes(width)
    mine = picked[pairs].astype(bf16)
    for g in range(pairs):
        here = picked[g]
        turned = pltpu.roll(here, half, 1)
        for odd in range(2):
            first, second = (turned, here) if odd else (here, turned)
            out_ref[2 * g + odd, 0:width] = mine
            out_ref[2 * g + odd, width : 2 * width] = jnp.where(lane < half, first, second).astype(
                bf16
            )


def pick(rows, hub_ids, feats):
    width, nodes = feats.shape
    domains, slots = rows.shape
    groups = domains // 2 + 1
    return pl.pallas_call(
        pick_kernel,
        out_shape=(
            jax.ShapeDtypeStruct((domains, 2 * width, edge), bf16),
            jax.ShapeDtypeStruct((groups, span, edge), bf16),
            jax.ShapeDtypeStruct((groups, edge), jnp.int32),
        ),
        in_specs=[hbm, hbm, hbm],
        out_specs=(vmem, vmem, vmem),
        scratch_shapes=[
            pltpu.VMEM((width, nodes), bf16),
            pltpu.VMEM((edge,), jnp.int32),
            pltpu.VMEM((domains, slots), jnp.int32),
            pltpu.VMEM((groups, edge), jnp.int32),
            pltpu.VMEM((nodes // span, width, span), bf16),
            pltpu.VMEM((groups, width, edge), f32),
            pltpu.SemaphoreType.DMA((3,)),
        ],
        compiler_params=params(32),
        name="pick",
    )(*far_off(rows, hub_ids, feats))


def deal_kernel(feats_ref, cotangent_ref, self_ref, neigh_ref, bias_ref, *rest):
    peers = len(rest) - 4
    outs, (w_self, w_neigh, bias, sems) = rest[:peers], rest[peers:]
    width, nodes = feats_ref.shape
    share = nodes // peers
    here = lax.axis_index("feat")
    small = [
        pltpu.make_async_copy(self_ref, w_self, sems.at[0]),
        pltpu.make_async_copy(neigh_ref, w_neigh, sems.at[1]),
        pltpu.make_async_copy(bias_ref, bias, sems.at[2]),
    ]
    large = []
    for k, out in enumerate(outs):
        there = pl.ds(pl.multiple_of((here ^ k) * share, share), share)
        for place, ref in enumerate((feats_ref, cotangent_ref)):
            large.append(
                pltpu.make_async_copy(
                    ref.at[:, there],
                    out.at[:, place * share : (place + 1) * share],
                    sems.at[3 + 2 * k + place],
                )
            )
    for copy in small + large:
        copy.start()
    for copy in small:
        copy.wait()
    square = (width, width)
    diagonal = lax.broadcasted_iota(jnp.int32, square, 0) == lax.broadcasted_iota(
        jnp.int32, square, 1
    )
    spread_bias = jnp.broadcast_to(bias[...].reshape(1, width), square)
    column = jnp.sum(jnp.where(diagonal, spread_bias, 0.0), axis=1, keepdims=True)
    block = column_block(column).astype(bf16)
    for out in outs:
        out[:, 2 * share : 2 * share + edge] = w_self[...]
        out[:, 2 * share + edge : 2 * share + 2 * edge] = w_neigh[...]
        out[:, 2 * share + 2 * edge : 2 * share + 3 * edge] = block
    for copy in large:
        copy.wait()


def deal(feats, cotangent, w_self, w_neigh, bias, peers):
    width, nodes = feats.shape
    part = jax.ShapeDtypeStruct((width, 2 * nodes // peers + 3 * edge), bf16)
    return pl.pallas_call(
        deal_kernel,
        out_shape=(part,) * peers,
        in_specs=[hbm] * 5,
        out_specs=(vmem,) * peers,
        scratch_shapes=[
            pltpu.VMEM((width, edge), bf16),
            pltpu.VMEM((width, edge), bf16),
            pltpu.VMEM((width,), f32),
            pltpu.SemaphoreType.DMA((3 + 2 * peers,)),
        ],
        compiler_params=params(32),
        name="deal",
    )(*far_off(feats, cotangent, w_self, w_neigh, bias))


def products_of(lefts, tiles, turned):
    results = []
    for i in range(0, len(tiles), 2):
        left = jnp.concatenate([lefts[i], lefts[i + 1]], axis=0)
        right = jnp.concatenate([tiles[i], tiles[i + 1]], axis=0 if turned else 1)
        contract = (((1,), (1 if turned else 0,)), ((), ()))
        both = lax.dot_general(left, right, contract, preferred_element_type=f32)
        width = lefts[i].shape[0]
        results += [both[:width, :edge], both[width:, edge:]]
    return results


def fetch(work, vals_ref, held, sems, start, stop):
    def some(k, carry):
        for i in range(group):
            tile = work[jnp.minimum(start + k * group + i, stop - 1)] & 511
            pltpu.make_async_copy(vals_ref.at[tile], held.at[k * group + i], sems.at[k]).start()
        return carry

    lax.fori_loop(0, (stop - start + group - 1) // group, some, 0)


def visit(work, vals_ref, held, sems, table, total, start, stop, turned):
    spare = total.shape[0] - 1

    def some(k, carry):
        slot = k * group
        first = start + slot
        lefts, tiles, places = [], [], []
        for i in range(group):
            code = work[jnp.minimum(first + i, stop - 1)]
            target = (code >> 9) & 511
            source = code >> 18
            lefts.append(table[source if turned else target])
            places.append(jnp.where(first + i < stop, target if turned else source, spare))
        pltpu.make_async_copy(
            vals_ref.at[pl.ds(0, group)], held.at[pl.ds(slot, group)], sems.at[k]
        ).wait()
        for i in range(group):
            tiles.append(held[slot + i])
        for place, product in zip(places, products_of(lefts, tiles, turned)):
            total[place] += product
        return carry

    lax.fori_loop(0, (stop - start + group - 1) // group, some, 0)


def own_kernel(
    dst_ref,
    src_ref,
    count_ref,
    feats_ref,
    vals_ref,
    total_ref,
    work_ref,
    dst,
    src,
    count,
    work,
    near,
    table,
    total,
    held,
    sems,
    tile_sems,
):
    width, nodes = feats_ref.shape
    own = nodes // edge
    tiles = vals_ref.shape[0]
    lists = [
        pltpu.make_async_copy(count_ref, count, sems.at[0]),
        pltpu.make_async_copy(dst_ref, dst, sems.at[1]),
        pltpu.make_async_copy(src_ref, src, sems.at[2]),
    ]
    for copy in lists:
        copy.start()
    features = pltpu.make_async_copy(feats_ref, near, sems.at[3])
    features.start()
    total[...] = jnp.zeros_like(total)
    lists[0].wait()
    live = count[0]
    for copy in lists[1:]:
        copy.wait()

    def sort(t, ends):
        low, high = ends
        source = src[t]
        far = source >= own
        work[jnp.where(far, high, low)] = t + (dst[t] << 9) + (source << 18)
        return jnp.where(far, low, low + 1), jnp.where(far, high - 1, high)

    middle, _ = lax.fori_loop(0, live, sort, (0, live - 1))
    work[tiles] = middle
    work[tiles + 1] = live
    record = pltpu.make_async_copy(work, work_ref, sems.at[4])
    record.start()
    fetch(work, vals_ref, held, tile_sems, 0, middle)
    features.wait()
    for b in range(own):
        table[b] = near[:, b * edge : (b + 1) * edge]

    visit(work, vals_ref, held, tile_sems, table, total, 0, middle, True)
    total_ref[...] = total[0:own]
    record.wait()


def own_tiles(dst, src, count, feats, vals):
    width, nodes = feats.shape
    own = nodes // edge
    tiles = vals.shape[0]
    return pl.pallas_call(
        own_kernel,
        out_shape=(
            jax.ShapeDtypeStruct((own, width, edge), f32),
            jax.ShapeDtypeStruct((tiles + edge,), jnp.int32),
        ),
        in_specs=[hbm] * 5,
        out_specs=(vmem, vmem),
        scratch_shapes=[
            pltpu.SMEM((tiles,), jnp.int32),
            pltpu.SMEM((tiles,), jnp.int32),
            pltpu.SMEM((1,), jnp.int32),
            pltpu.SMEM((tiles + edge,), jnp.int32),
            pltpu.VMEM((width, nodes), bf16),
            pltpu.VMEM((own, width, edge), bf16),
            pltpu.VMEM((own + 1, width, edge), f32),
            pltpu.VMEM((tiles, edge, edge), bf16),
            pltpu.SemaphoreType.DMA((5,)),
            pltpu.SemaphoreType.DMA((tiles // group,)),
        ],
        compiler_params=params(32),
        name="own_tiles",
    )(*far_off(dst, src), count, *far_off(feats, vals))


def far_kernel(work, recv_ref, begun_ref, vals_ref, out_ref, table, total, held, tile_sems):
    own, width, _ = begun_ref.shape
    domains = recv_ref.shape[0]
    peers = out_ref.shape[0]
    tiles = vals_ref.shape[0]
    start, stop = work[tiles], work[tiles + 1]
    fetch(work, vals_ref, held, tile_sems, start, stop)
    lane = lanes(width)
    for g in range(domains // 2):
        table[own + g] = jnp.where(
            lane < edge // 2,
            recv_ref[2 * g, width : 2 * width].astype(f32),
            recv_ref[2 * g + 1, width : 2 * width].astype(f32),
        ).astype(bf16)
    for q in range(domains):
        table[own + domains // 2 + q] = recv_ref[q, 0:width]
    total[0:own] = begun_ref[...]
    visit(work, vals_ref, held, tile_sems, table, total, start, stop, True)
    per = own // peers
    for b in range(own):
        col = (b % per) * edge
        out_ref[b // per, :, col : col + edge] = total[b].astype(bf16)


def far_tiles(work, recv, begun, vals, peers):
    own, width, _ = begun.shape
    domains = recv.shape[0]
    nodes = own * edge
    tiles = vals.shape[0]
    return pl.pallas_call(
        far_kernel,
        out_shape=jax.ShapeDtypeStruct((peers, width, nodes // peers), bf16),
        in_specs=[smem, vmem, vmem, hbm],
        out_specs=vmem,
        scratch_shapes=[
            pltpu.VMEM((own + domains // 2 + domains, width, edge), bf16),
            pltpu.VMEM((own + 1, width, edge), f32),
            pltpu.VMEM((tiles, edge, edge), bf16),
            pltpu.SemaphoreType.DMA((tiles // group,)),
        ],
        compiler_params=params(32),
        name="far_tiles",
    )(work, recv, begun, *far_off(vals))


def fill_blocks(near_ref, blocks):
    own = blocks.shape[0]
    per = own // near_ref.shape[0]
    for b in range(own):
        col = (b % per) * edge
        blocks[b] = near_ref[b // per, :, col : col + edge]


def away_kernel(work, near_ref, vals_ref, out_ref, blocks, total, held, tile_sems):
    peers, width, _ = near_ref.shape
    own = blocks.shape[0]
    share = own // peers * edge
    domains = out_ref.shape[0]
    far = own + domains // 2
    tiles = vals_ref.shape[0]
    start, stop = work[tiles], work[tiles + 1]
    fetch(work, vals_ref, held, tile_sems, start, stop)
    fill_blocks(near_ref, blocks)
    total[...] = jnp.zeros_like(total)

    def summed(place):
        start = share + place * edge
        return jnp.sum(near_ref[:, :, start : start + edge].astype(f32), axis=0)

    grad_self = summed(0).astype(bf16)
    grad_neigh = summed(1).astype(bf16)
    grad_bias = column_block(jnp.sum(summed(2), axis=1, keepdims=True))
    grad_bias = pltpu.roll(grad_bias, edge // 2, 1)
    visit(work, vals_ref, held, tile_sems, blocks, total, start, stop, False)
    lane = lanes(width)
    for g in range(domains // 2):
        here = total[own + g]
        for odd in range(2):
            q = 2 * g + odd
            mine = pltpu.roll(here, edge // 2, 1) if odd else here
            out_ref[q, 0:width] = total[far + q].astype(bf16)
            out_ref[q, width : 2 * width] = jnp.where(lane < edge // 2, mine, grad_bias).astype(bf16)
            out_ref[q, 2 * width : 3 * width] = grad_self
            out_ref[q, 3 * width : 4 * width] = grad_neigh


def away(work, near, vals, domains, nodes):
    _, width, _ = near.shape
    tiles = vals.shape[0]
    own = nodes // edge
    return pl.pallas_call(
        away_kernel,
        out_shape=jax.ShapeDtypeStruct((domains, 4 * width, edge), bf16),
        in_specs=[smem, vmem, hbm],
        out_specs=vmem,
        scratch_shapes=[
            pltpu.VMEM((own, width, edge), bf16),
            pltpu.VMEM((own + domains // 2 + domains + 1, width, edge), f32),
            pltpu.VMEM((tiles, edge, edge), bf16),
            pltpu.SemaphoreType.DMA((tiles // group,)),
        ],
        compiler_params=params(32),
        name="away",
    )(work, near, *far_off(vals))


def home_kernel(work, near_ref, vals_ref, out_ref, blocks, total, held, tile_sems):
    own = blocks.shape[0]
    tiles = vals_ref.shape[0]
    stop = work[tiles]
    fetch(work, vals_ref, held, tile_sems, 0, stop)
    fill_blocks(near_ref, blocks)
    total[...] = jnp.zeros_like(total)
    visit(work, vals_ref, held, tile_sems, blocks, total, 0, stop, False)
    for b in range(own):
        out_ref[:, b * edge : (b + 1) * edge] = total[b]


def home(work, near, vals, nodes):
    _, width, _ = near.shape
    tiles = vals.shape[0]
    own = nodes // edge
    return pl.pallas_call(
        home_kernel,
        out_shape=jax.ShapeDtypeStruct((width, nodes), f32),
        in_specs=[smem, vmem, hbm],
        out_specs=vmem,
        scratch_shapes=[
            pltpu.VMEM((own, width, edge), bf16),
            pltpu.VMEM((own + 1, width, edge), f32),
            pltpu.VMEM((tiles, edge, edge), bf16),
            pltpu.SemaphoreType.DMA((tiles // group,)),
        ],
        compiler_params=params(32),
        name="home",
    )(work, near, *far_off(vals))


def layer_kernel(agg_ref, *rest):
    peers, width, share = agg_ref.shape
    rows = peers * width
    parts, near_ref, lates = rest[:peers], rest[peers], rest[peers + 1 : 2 * peers + 1]
    feats_all, cotangent_all, self_all, neigh_all, bias_all, act, back = rest[2 * peers + 1 :]
    here = lax.axis_index("feat")
    for k, part in enumerate(parts):
        peer = here ^ k
        feats_all[peer] = part[:, 0:share]
        cotangent_all[peer] = part[:, share : 2 * share]
        self_all[peer] = part[:, 2 * share : 2 * share + edge]
        neigh_all[peer] = part[:, 2 * share + edge : 2 * share + 2 * edge]
        bias_all[peer] = part[:, 2 * share + 2 * edge : 2 * share + 3 * edge]
    feats = feats_all[...].reshape(rows, share)
    cotangent = cotangent_all[...].reshape(rows, share)
    w_self = self_all[...].reshape(rows, edge)
    w_neigh = neigh_all[...].reshape(rows, edge)
    bias = jnp.sum(bias_all[...].reshape(rows, edge).astype(f32), axis=1, keepdims=True)
    aggregate = agg_ref[...].reshape(rows, share)
    first = (((0,), (0,)), ((), ()))
    last = (((1,), (1,)), ((), ()))
    linear = lax.dot_general(w_self, feats, first, preferred_element_type=f32)
    linear = linear + lax.dot_general(w_neigh, aggregate, first, preferred_element_type=f32)
    linear = linear + bias
    logistic = jax.nn.sigmoid(linear)
    act[...] = (linear * logistic).astype(bf16).reshape(peers, width, share)
    slope = logistic * (1.0 + linear * (1.0 - logistic))
    grad = (cotangent.astype(f32) * slope).astype(bf16)
    near_ref[:, :, 0:share] = (
        jnp.dot(w_neigh, grad, preferred_element_type=f32).astype(bf16).reshape(peers, width, share)
    )
    back[...] = (
        jnp.dot(w_self, grad, preferred_element_type=f32).astype(bf16).reshape(peers, width, share)
    )
    grad_self = lax.dot_general(feats, grad, last, preferred_element_type=f32)
    grad_neigh = lax.dot_general(aggregate, grad, last, preferred_element_type=f32)
    grad_bias = column_block(jnp.sum(grad.astype(f32), axis=1, keepdims=True)).astype(bf16)
    for place, piece in enumerate((grad_self.astype(bf16), grad_neigh.astype(bf16), grad_bias)):
        start = share + place * edge
        near_ref[:, :, start : start + edge] = piece.reshape(peers, width, edge)
    for k, late in enumerate(lates):
        peer = here ^ k
        late[:, 0:share] = act[peer]
        late[:, share : 2 * share] = back[peer]


def layer(agg, parts):
    peers, width, share = agg.shape
    return pl.pallas_call(
        layer_kernel,
        out_shape=(jax.ShapeDtypeStruct((peers, width, share + 3 * edge), bf16),)
        + (jax.ShapeDtypeStruct((width, 2 * share), bf16),) * peers,
        in_specs=[vmem] * (1 + peers),
        out_specs=(vmem,) * (1 + peers),
        scratch_shapes=[
            pltpu.VMEM((peers, width, share), bf16),
            pltpu.VMEM((peers, width, share), bf16),
            pltpu.VMEM((peers, width, edge), bf16),
            pltpu.VMEM((peers, width, edge), bf16),
            pltpu.VMEM((peers, width, edge), bf16),
            pltpu.VMEM((peers, width, share), bf16),
            pltpu.VMEM((peers, width, share), bf16),
        ],
        compiler_params=params(32),
        name="layer",
    )(agg, *parts)


def settle_kernel(scale, home_ref, hot_ref, recv_ref, base_ref, *rest):
    width, nodes = base_ref.shape
    lates, rest = rest[:-8], rest[-8:]
    act_ref, feats_ref, self_ref, neigh_ref, bias_ref, marked, hots, back = rest
    domains = recv_ref.shape[0]
    peers = len(lates)
    share = nodes // peers
    count = nodes // span
    pairs = domains // 2
    here = lax.axis_index("feat")
    for k, late in enumerate(lates):
        peer = here ^ k
        act_ref[:, pl.ds(pl.multiple_of(peer * share, share), share)] = late[:, 0:share]
        back[:, pl.ds(pl.multiple_of(peer * share, share), share)] = late[:, share : 2 * share]
    lane = lanes(width)

    def over(start):
        return jnp.sum(recv_ref[:, start : start + width].astype(f32), axis=0)

    hub = over(0)
    self_ref[...] = over(2 * width) * scale
    neigh_ref[...] = over(3 * width) * scale
    tail = jnp.where(lane >= edge // 2, over(width), 0.0)
    column = jnp.broadcast_to(jnp.sum(tail, axis=1, keepdims=True) * scale, (width, edge))
    row = lax.broadcasted_iota(jnp.int32, (width, edge), 0)
    bias_ref[...] = jnp.sum(jnp.where(row == lane, column, 0.0), axis=0)[:width]
    hub_pieces = split(hub, 3)
    for g in range(pairs + 3):
        if g < pairs:
            first = recv_ref[2 * g, width : 2 * width].astype(f32)
            second = pltpu.roll(recv_ref[2 * g + 1, width : 2 * width].astype(f32), edge // 2, 1)
            value = jnp.where(lane < edge // 2, first, second)
        else:
            value = hub_pieces[g - pairs].astype(f32)
        at = min(g, pairs)
        where = jnp.broadcast_to(home_ref[at : at + 1, :], (width, edge))
        hots[:, g * edge : (g + 1) * edge] = hot_ref[at]
        for b in range(count):
            marked[b * width : (b + 1) * width, g * edge : (g + 1) * edge] = jnp.where(
                where == b, value, 0.0
            ).astype(bf16)
    placed = lax.dot_general(
        marked[...], hots[...], (((1,), (1,)), ((), ())), preferred_element_type=f32
    )
    for b in range(count):
        cols = slice(b * span, (b + 1) * span)
        feats_ref[:, cols] = (
            back[:, cols].astype(f32) + base_ref[:, cols] + placed[b * width : (b + 1) * width]
        ).astype(bf16)


def settle(homes, hot, recv, base, lates, scale):
    width, nodes = base.shape
    domains = recv.shape[0]
    terms = (domains // 2 + 3) * edge
    return pl.pallas_call(
        functools.partial(settle_kernel, scale),
        out_shape=(
            jax.ShapeDtypeStruct((width, nodes), bf16),
            jax.ShapeDtypeStruct((width, nodes), bf16),
            jax.ShapeDtypeStruct((width, edge), f32),
            jax.ShapeDtypeStruct((width, edge), f32),
            jax.ShapeDtypeStruct((width,), f32),
        ),
        in_specs=[vmem] * (4 + len(lates)),
        out_specs=(vmem,) * 5,
        scratch_shapes=[
            pltpu.VMEM((nodes // span * width, terms), bf16),
            pltpu.VMEM((span, terms), bf16),
            pltpu.VMEM((width, nodes), bf16),
        ],
        compiler_params=params(32),
        name="settle",
    )(homes, hot, recv, base, *lates)


def swap(values, axis):
    return lax.all_to_all(values, axis, split_axis=0, concat_axis=0, tiled=True)


def trade(parts, axis):
    peers = len(parts)
    return [
        part if k == 0 else lax.ppermute(part, axis, [(i, i ^ k) for i in range(peers)])
        for k, part in enumerate(parts)
    ]


def local(
    feats,
    tile_vals,
    tile_dst,
    tile_src,
    tile_count,
    send_rows,
    hub_ids,
    w_self,
    w_neigh,
    bias,
    cotangent,
):
    nodes = feats.shape[1]
    domains = lax.axis_size("dom")
    peers = lax.axis_size("feat")
    picked, hot, homes = pick(send_rows[0], hub_ids, feats)
    picked, bias = lax.optimization_barrier((picked, bias))
    recv = swap(picked, "dom")
    parts = trade(deal(feats, cotangent, w_self, w_neigh, bias, peers), "feat")
    begun, work = own_tiles(tile_dst, tile_src, tile_count, feats, tile_vals)
    recv, parts = lax.optimization_barrier((recv, parts))
    agg = swap(far_tiles(work, recv, begun, tile_vals, peers), "feat")
    near, *lates = layer(agg, parts)
    near = swap(near, "feat")
    back = away(work, near, tile_vals, domains, nodes)
    back, lates = lax.optimization_barrier((back, lates))
    back = swap(back, "dom")
    lates = trade(lates, "feat")
    base = home(work, near, tile_vals, nodes)
    scale = 1.0 / math.sqrt(nodes * domains)
    return settle(homes, hot, back, base, lates, scale)


def solution(mesh):
    placed = (
        P("feat", "dom"),
        P("dom", None, None),
        P("dom"),
        P("dom"),
        P("dom"),
        P("dom", None, None),
        P("dom"),
        P("feat", None),
        P("feat", None),
        P("feat"),
        P("feat", "dom"),
    )
    return jax.shard_map(
        local,
        mesh=mesh,
        in_specs=placed,
        out_specs=(P("feat", "dom"), P("feat", "dom"), P("feat", None), P("feat", None), P("feat")),
        check_vma=False,
    )
```

```python
import functools
import math

import jax
import jax.numpy as jnp
from jax import lax
from jax.experimental import pallas as pl
from jax.experimental.pallas import tpu as pltpu
from jax.sharding import PartitionSpec as P

edge = 128
span = 256
group = 32
bf16 = jnp.bfloat16
f32 = jnp.float32
vmem = pl.BlockSpec(memory_space=pltpu.VMEM)
smem = pl.BlockSpec(memory_space=pltpu.SMEM)
hbm = pl.BlockSpec(memory_space=pl.ANY)


def params(mib):
    return pltpu.CompilerParams(vmem_limit_bytes=mib * 1024 * 1024)


def far_off(*values):
    return [pltpu.with_memory_space_constraint(value, pltpu.HBM) for value in values]


def lanes(rows):
    return lax.broadcasted_iota(jnp.int32, (rows, edge), 1)


def split(values, pieces):
    parts = []
    for _ in range(pieces):
        part = values.astype(bf16)
        parts.append(part)
        values = values - part.astype(f32)
    return parts


def column_block(column):
    hi, mid, lo = split(column, 3)
    lane = lanes(column.shape[0])
    block = jnp.where(lane == 0, hi.astype(f32), 0.0)
    block = jnp.where(lane == 1, mid.astype(f32), block)
    return jnp.where(lane == 2, lo.astype(f32), block)


def pick_kernel(
    rows_ref, hub_ref, feats_ref, out_ref, hot_ref, home_ref, near, hub, wide, index, blocks, picked, sems
):
    width, nodes = feats_ref.shape
    count = nodes // span
    pairs = rows_ref.shape[0] // 2
    half = edge // 2
    copies = [
        pltpu.make_async_copy(feats_ref, near, sems.at[0]),
        pltpu.make_async_copy(rows_ref, wide, sems.at[1]),
        pltpu.make_async_copy(hub_ref, hub, sems.at[2]),
    ]
    for copy in copies:
        copy.start()
    copies[1].wait()
    copies[2].wait()
    lane = lanes(1)
    for g in range(pairs):
        row = jnp.concatenate([wide[2 * g : 2 * g + 1, :], wide[2 * g + 1 : 2 * g + 2, :]], axis=1)
        index[g : g + 1, :] = row
    index[pairs : pairs + 1, :] = hub[...].reshape(1, edge)
    home_ref[...] = index[...] >> 8
    copies[0].wait()
    for b in range(count):
        blocks[b] = near[:, b * span : (b + 1) * span]
    sub = lax.broadcasted_iota(jnp.int32, (span, edge), 0)

    def step(g, carry):
        place = index[pl.ds(g, 1), :] & (span - 1)
        home = jnp.broadcast_to(home_ref[pl.ds(g, 1), :], (width, edge))
        hot = jnp.where(sub == place, 1.0, 0.0).astype(bf16)
        hot_ref[g] = hot
        found = jnp.dot(blocks[...].reshape(count * width, span), hot, preferred_element_type=f32)
        total = found[0:width]
        for b in range(1, count):
            total = jnp.where(home == b, found[b * width : (b + 1) * width], total)
        picked[g] = total
        return carry

    lax.fori_loop(0, pairs, step, 0, unroll=4)
    step(pairs, 0)
    lane = lanes(width)
    mine = picked[pairs].astype(bf16)
    for g in range(pairs):
        here = picked[g]
        turned = pltpu.roll(here, half, 1)
        for odd in range(2):
            first, second = (turned, here) if odd else (here, turned)
            out_ref[2 * g + odd, 0:width] = mine
            out_ref[2 * g + odd, width : 2 * width] = jnp.where(lane < half, first, second).astype(
                bf16
            )


def pick(rows, hub_ids, feats):
    width, nodes = feats.shape
    domains, slots = rows.shape
    groups = domains // 2 + 1
    return pl.pallas_call(
        pick_kernel,
        out_shape=(
            jax.ShapeDtypeStruct((domains, 2 * width, edge), bf16),
            jax.ShapeDtypeStruct((groups, span, edge), bf16),
            jax.ShapeDtypeStruct((groups, edge), jnp.int32),
        ),
        in_specs=[hbm, hbm, hbm],
        out_specs=(vmem, vmem, vmem),
        scratch_shapes=[
            pltpu.VMEM((width, nodes), bf16),
            pltpu.VMEM((edge,), jnp.int32),
            pltpu.VMEM((domains, slots), jnp.int32),
            pltpu.VMEM((groups, edge), jnp.int32),
            pltpu.VMEM((nodes // span, width, span), bf16),
            pltpu.VMEM((groups, width, edge), f32),
            pltpu.SemaphoreType.DMA((3,)),
        ],
        compiler_params=params(32),
        name="pick",
    )(*far_off(rows, hub_ids, feats))


def deal_kernel(feats_ref, cotangent_ref, self_ref, neigh_ref, bias_ref, *rest):
    peers = len(rest) - 4
    outs, (w_self, w_neigh, bias, sems) = rest[:peers], rest[peers:]
    width, nodes = feats_ref.shape
    share = nodes // peers
    here = lax.axis_index("feat")
    small = [
        pltpu.make_async_copy(self_ref, w_self, sems.at[0]),
        pltpu.make_async_copy(neigh_ref, w_neigh, sems.at[1]),
        pltpu.make_async_copy(bias_ref, bias, sems.at[2]),
    ]
    large = []
    for k, out in enumerate(outs):
        there = pl.ds(pl.multiple_of((here ^ k) * share, share), share)
        for place, ref in enumerate((feats_ref, cotangent_ref)):
            large.append(
                pltpu.make_async_copy(
                    ref.at[:, there],
                    out.at[:, place * share : (place + 1) * share],
                    sems.at[3 + 2 * k + place],
                )
            )
    for copy in small + large:
        copy.start()
    for copy in small:
        copy.wait()
    square = (width, width)
    diagonal = lax.broadcasted_iota(jnp.int32, square, 0) == lax.broadcasted_iota(
        jnp.int32, square, 1
    )
    spread_bias = jnp.broadcast_to(bias[...].reshape(1, width), square)
    column = jnp.sum(jnp.where(diagonal, spread_bias, 0.0), axis=1, keepdims=True)
    block = column_block(column).astype(bf16)
    for out in outs:
        out[:, 2 * share : 2 * share + edge] = w_self[...]
        out[:, 2 * share + edge : 2 * share + 2 * edge] = w_neigh[...]
        out[:, 2 * share + 2 * edge : 2 * share + 3 * edge] = block
    for copy in large:
        copy.wait()


def deal(feats, cotangent, w_self, w_neigh, bias, peers):
    width, nodes = feats.shape
    part = jax.ShapeDtypeStruct((width, 2 * nodes // peers + 3 * edge), bf16)
    return pl.pallas_call(
        deal_kernel,
        out_shape=(part,) * peers,
        in_specs=[hbm] * 5,
        out_specs=(vmem,) * peers,
        scratch_shapes=[
            pltpu.VMEM((width, edge), bf16),
            pltpu.VMEM((width, edge), bf16),
            pltpu.VMEM((width,), f32),
            pltpu.SemaphoreType.DMA((3 + 2 * peers,)),
        ],
        compiler_params=params(32),
        name="deal",
    )(*far_off(feats, cotangent, w_self, w_neigh, bias))


def products_of(lefts, tiles, turned):
    results = []
    for i in range(0, len(tiles), 2):
        left = jnp.concatenate([lefts[i], lefts[i + 1]], axis=0)
        right = jnp.concatenate([tiles[i], tiles[i + 1]], axis=0 if turned else 1)
        contract = (((1,), (1 if turned else 0,)), ((), ()))
        both = lax.dot_general(left, right, contract, preferred_element_type=f32)
        width = lefts[i].shape[0]
        results += [both[:width, :edge], both[width:, edge:]]
    return results


def walk_tiles(refs, scratch, prepare, table, total, own):
    dst_ref, src_ref, count_ref, vals_ref = refs
    dst, src, count, work, held, sems, tile_sems = scratch
    slots = dst.shape[0]
    spare = total.shape[0] - 1
    lists = [
        pltpu.make_async_copy(count_ref, count, sems.at[0]),
        pltpu.make_async_copy(dst_ref, dst, sems.at[1]),
        pltpu.make_async_copy(src_ref, src, sems.at[2]),
    ]

    def fetch(k):
        rows = pl.ds(k * group, group)
        return pltpu.make_async_copy(vals_ref.at[rows], held.at[rows], tile_sems.at[k])

    def begin(k, carry):
        fetch(k).start()
        return carry

    for copy in lists:
        copy.start()
    lists[0].wait()
    live = count[0]
    groups = (live + group - 1) // group
    lax.fori_loop(0, groups, begin, 0)
    prepare()
    for copy in lists[1:]:
        copy.wait()

    def some(k, ends):
        low, high = ends
        first = k * group
        lefts, places = [], []
        for i in range(group):
            t = first + i
            target, source = dst[t], src[t]
            alive, far = t < live, source >= own
            lefts.append(table[source])
            places.append(jnp.where(alive, target, spare))
            entry = jnp.where(alive, jnp.where(far, high, low), slots + 2)
            work[entry] = t + (target << 9) + (source << 18)
            low = low + jnp.where(alive & ~far, 1, 0)
            high = high - jnp.where(alive & far, 1, 0)
        fetch(k).wait()
        tiles = [held[first + i] for i in range(group)]
        for place, product in zip(places, products_of(lefts, tiles, True)):
            total[place] += product
        return low, high

    middle, _ = lax.fori_loop(0, groups, some, (0, live - 1))
    work[slots] = middle
    work[slots + 1] = live


def tile_scratch(tiles):
    return [
        pltpu.SMEM((tiles,), jnp.int32),
        pltpu.SMEM((tiles,), jnp.int32),
        pltpu.SMEM((1,), jnp.int32),
        pltpu.SMEM((tiles + edge,), jnp.int32),
        pltpu.VMEM((tiles, edge, edge), bf16),
        pltpu.SemaphoreType.DMA((3,)),
        pltpu.SemaphoreType.DMA((tiles // group,)),
    ]


def gather_kernel(
    dst_ref,
    src_ref,
    count_ref,
    vals_ref,
    feats_ref,
    recv_ref,
    out_ref,
    work_ref,
    near,
    table,
    total,
    sems,
    *scratch,
):
    width, nodes = feats_ref.shape
    own = nodes // edge
    domains = recv_ref.shape[0]
    peers = out_ref.shape[0]
    features = pltpu.make_async_copy(feats_ref, near, sems.at[0])
    features.start()

    def prepare():
        lane = lanes(width)
        for g in range(domains // 2):
            table[own + g] = jnp.where(
                lane < edge // 2,
                recv_ref[2 * g, width : 2 * width].astype(f32),
                recv_ref[2 * g + 1, width : 2 * width].astype(f32),
            ).astype(bf16)
        for q in range(domains):
            table[own + domains // 2 + q] = recv_ref[q, 0:width]
        total[...] = jnp.zeros_like(total)
        features.wait()
        for b in range(own):
            table[b] = near[:, b * edge : (b + 1) * edge]

    walk_tiles((dst_ref, src_ref, count_ref, vals_ref), scratch, prepare, table, total, own)
    record = pltpu.make_async_copy(scratch[3], work_ref, sems.at[1])
    record.start()
    per = own // peers
    for b in range(own):
        col = (b % per) * edge
        out_ref[b // per, :, col : col + edge] = total[b].astype(bf16)
    record.wait()


def gather(dst, src, count, vals, feats, recv, peers):
    width, nodes = feats.shape
    own = nodes // edge
    domains = recv.shape[0]
    return pl.pallas_call(
        gather_kernel,
        out_shape=(
            jax.ShapeDtypeStruct((peers, width, nodes // peers), bf16),
            jax.ShapeDtypeStruct((dst.shape[0] + edge,), jnp.int32),
        ),
        in_specs=[hbm] * 5 + [vmem],
        out_specs=(vmem, vmem),
        scratch_shapes=[
            pltpu.VMEM((width, nodes), bf16),
            pltpu.VMEM((own + domains // 2 + domains, width, edge), bf16),
            pltpu.VMEM((own + 1, width, edge), f32),
            pltpu.SemaphoreType.DMA((2,)),
        ]
        + tile_scratch(vals.shape[0]),
        compiler_params=params(32),
        name="gather",
    )(*far_off(dst, src), count, *far_off(vals, feats), recv)


def fetch(work, vals_ref, held, sems, start, stop):
    def some(k, carry):
        for i in range(group):
            tile = work[jnp.minimum(start + k * group + i, stop - 1)] & 511
            pltpu.make_async_copy(vals_ref.at[tile], held.at[k * group + i], sems.at[k]).start()
        return carry

    lax.fori_loop(0, (stop - start + group - 1) // group, some, 0)


def visit(work, vals_ref, held, sems, table, total, start, stop, turned):
    spare = total.shape[0] - 1

    def some(k, carry):
        slot = k * group
        first = start + slot
        lefts, tiles, places = [], [], []
        for i in range(group):
            code = work[jnp.minimum(first + i, stop - 1)]
            target = (code >> 9) & 511
            source = code >> 18
            lefts.append(table[source if turned else target])
            places.append(jnp.where(first + i < stop, target if turned else source, spare))
        pltpu.make_async_copy(
            vals_ref.at[pl.ds(0, group)], held.at[pl.ds(slot, group)], sems.at[k]
        ).wait()
        for i in range(group):
            tiles.append(held[slot + i])
        for place, product in zip(places, products_of(lefts, tiles, turned)):
            total[place] += product
        return carry

    lax.fori_loop(0, (stop - start + group - 1) // group, some, 0)


def fill_blocks(near_ref, blocks):
    own = blocks.shape[0]
    per = own // near_ref.shape[0]
    for b in range(own):
        col = (b % per) * edge
        blocks[b] = near_ref[b // per, :, col : col + edge]


def away_kernel(work, near_ref, vals_ref, out_ref, blocks, total, held, tile_sems):
    peers, width, _ = near_ref.shape
    own = blocks.shape[0]
    share = own // peers * edge
    domains = out_ref.shape[0]
    far = own + domains // 2
    tiles = vals_ref.shape[0]
    start, stop = work[tiles], work[tiles + 1]
    fetch(work, vals_ref, held, tile_sems, start, stop)
    fill_blocks(near_ref, blocks)
    total[...] = jnp.zeros_like(total)

    def summed(place):
        start = share + place * edge
        return jnp.sum(near_ref[:, :, start : start + edge].astype(f32), axis=0)

    grad_self = summed(0).astype(bf16)
    grad_neigh = summed(1).astype(bf16)
    grad_bias = column_block(jnp.sum(summed(2), axis=1, keepdims=True))
    grad_bias = pltpu.roll(grad_bias, edge // 2, 1)
    visit(work, vals_ref, held, tile_sems, blocks, total, start, stop, False)
    lane = lanes(width)
    for g in range(domains // 2):
        here = total[own + g]
        for odd in range(2):
            q = 2 * g + odd
            mine = pltpu.roll(here, edge // 2, 1) if odd else here
            out_ref[q, 0:width] = total[far + q].astype(bf16)
            out_ref[q, width : 2 * width] = jnp.where(lane < edge // 2, mine, grad_bias).astype(bf16)
            out_ref[q, 2 * width : 3 * width] = grad_self
            out_ref[q, 3 * width : 4 * width] = grad_neigh


def away(work, near, vals, domains, nodes):
    _, width, _ = near.shape
    tiles = vals.shape[0]
    own = nodes // edge
    return pl.pallas_call(
        away_kernel,
        out_shape=jax.ShapeDtypeStruct((domains, 4 * width, edge), bf16),
        in_specs=[smem, vmem, hbm],
        out_specs=vmem,
        scratch_shapes=[
            pltpu.VMEM((own, width, edge), bf16),
            pltpu.VMEM((own + domains // 2 + domains + 1, width, edge), f32),
            pltpu.VMEM((tiles, edge, edge), bf16),
            pltpu.SemaphoreType.DMA((tiles // group,)),
        ],
        compiler_params=params(32),
        name="away",
    )(work, near, *far_off(vals))


def home_kernel(work, near_ref, vals_ref, out_ref, blocks, total, held, tile_sems):
    own = blocks.shape[0]
    tiles = vals_ref.shape[0]
    stop = work[tiles]
    fetch(work, vals_ref, held, tile_sems, 0, stop)
    fill_blocks(near_ref, blocks)
    total[...] = jnp.zeros_like(total)
    visit(work, vals_ref, held, tile_sems, blocks, total, 0, stop, False)
    for b in range(own):
        out_ref[:, b * edge : (b + 1) * edge] = total[b]


def home(work, near, vals, nodes):
    _, width, _ = near.shape
    tiles = vals.shape[0]
    own = nodes // edge
    return pl.pallas_call(
        home_kernel,
        out_shape=jax.ShapeDtypeStruct((width, nodes), f32),
        in_specs=[smem, vmem, hbm],
        out_specs=vmem,
        scratch_shapes=[
            pltpu.VMEM((own, width, edge), bf16),
            pltpu.VMEM((own + 1, width, edge), f32),
            pltpu.VMEM((tiles, edge, edge), bf16),
            pltpu.SemaphoreType.DMA((tiles // group,)),
        ],
        compiler_params=params(32),
        name="home",
    )(work, near, *far_off(vals))


def layer_kernel(agg_ref, *rest):
    peers, width, share = agg_ref.shape
    rows = peers * width
    parts, near_ref, lates = rest[:peers], rest[peers], rest[peers + 1 : 2 * peers + 1]
    feats_all, cotangent_all, self_all, neigh_all, bias_all, act, back = rest[2 * peers + 1 :]
    here = lax.axis_index("feat")
    for k, part in enumerate(parts):
        peer = here ^ k
        feats_all[peer] = part[:, 0:share]
        cotangent_all[peer] = part[:, share : 2 * share]
        self_all[peer] = part[:, 2 * share : 2 * share + edge]
        neigh_all[peer] = part[:, 2 * share + edge : 2 * share + 2 * edge]
        bias_all[peer] = part[:, 2 * share + 2 * edge : 2 * share + 3 * edge]
    feats = feats_all[...].reshape(rows, share)
    cotangent = cotangent_all[...].reshape(rows, share)
    w_self = self_all[...].reshape(rows, edge)
    w_neigh = neigh_all[...].reshape(rows, edge)
    bias = jnp.sum(bias_all[...].reshape(rows, edge).astype(f32), axis=1, keepdims=True)
    aggregate = agg_ref[...].reshape(rows, share)
    first = (((0,), (0,)), ((), ()))
    last = (((1,), (1,)), ((), ()))
    linear = lax.dot_general(w_self, feats, first, preferred_element_type=f32)
    linear = linear + lax.dot_general(w_neigh, aggregate, first, preferred_element_type=f32)
    linear = linear + bias
    logistic = jax.nn.sigmoid(linear)
    act[...] = (linear * logistic).astype(bf16).reshape(peers, width, share)
    slope = logistic * (1.0 + linear * (1.0 - logistic))
    grad = (cotangent.astype(f32) * slope).astype(bf16)
    near_ref[:, :, 0:share] = (
        jnp.dot(w_neigh, grad, preferred_element_type=f32).astype(bf16).reshape(peers, width, share)
    )
    back[...] = (
        jnp.dot(w_self, grad, preferred_element_type=f32).astype(bf16).reshape(peers, width, share)
    )
    grad_self = lax.dot_general(feats, grad, last, preferred_element_type=f32)
    grad_neigh = lax.dot_general(aggregate, grad, last, preferred_element_type=f32)
    grad_bias = column_block(jnp.sum(grad.astype(f32), axis=1, keepdims=True)).astype(bf16)
    for place, piece in enumerate((grad_self.astype(bf16), grad_neigh.astype(bf16), grad_bias)):
        start = share + place * edge
        near_ref[:, :, start : start + edge] = piece.reshape(peers, width, edge)
    for k, late in enumerate(lates):
        peer = here ^ k
        late[:, 0:share] = act[peer]
        late[:, share : 2 * share] = back[peer]


def layer(agg, parts):
    peers, width, share = agg.shape
    return pl.pallas_call(
        layer_kernel,
        out_shape=(jax.ShapeDtypeStruct((peers, width, share + 3 * edge), bf16),)
        + (jax.ShapeDtypeStruct((width, 2 * share), bf16),) * peers,
        in_specs=[vmem] * (1 + peers),
        out_specs=(vmem,) * (1 + peers),
        scratch_shapes=[
            pltpu.VMEM((peers, width, share), bf16),
            pltpu.VMEM((peers, width, share), bf16),
            pltpu.VMEM((peers, width, edge), bf16),
            pltpu.VMEM((peers, width, edge), bf16),
            pltpu.VMEM((peers, width, edge), bf16),
            pltpu.VMEM((peers, width, share), bf16),
            pltpu.VMEM((peers, width, share), bf16),
        ],
        compiler_params=params(32),
        name="layer",
    )(agg, *parts)


def settle_kernel(scale, home_ref, hot_ref, recv_ref, base_ref, *rest):
    width, nodes = base_ref.shape
    lates, rest = rest[:-8], rest[-8:]
    act_ref, feats_ref, self_ref, neigh_ref, bias_ref, marked, hots, back = rest
    domains = recv_ref.shape[0]
    peers = len(lates)
    share = nodes // peers
    count = nodes // span
    pairs = domains // 2
    here = lax.axis_index("feat")
    for k, late in enumerate(lates):
        peer = here ^ k
        act_ref[:, pl.ds(pl.multiple_of(peer * share, share), share)] = late[:, 0:share]
        back[:, pl.ds(pl.multiple_of(peer * share, share), share)] = late[:, share : 2 * share]
    lane = lanes(width)

    def over(start):
        return jnp.sum(recv_ref[:, start : start + width].astype(f32), axis=0)

    hub = over(0)
    self_ref[...] = over(2 * width) * scale
    neigh_ref[...] = over(3 * width) * scale
    tail = jnp.where(lane >= edge // 2, over(width), 0.0)
    column = jnp.broadcast_to(jnp.sum(tail, axis=1, keepdims=True) * scale, (width, edge))
    row = lax.broadcasted_iota(jnp.int32, (width, edge), 0)
    bias_ref[...] = jnp.sum(jnp.where(row == lane, column, 0.0), axis=0)[:width]
    hub_pieces = split(hub, 3)
    for g in range(pairs + 3):
        if g < pairs:
            first = recv_ref[2 * g, width : 2 * width].astype(f32)
            second = pltpu.roll(recv_ref[2 * g + 1, width : 2 * width].astype(f32), edge // 2, 1)
            value = jnp.where(lane < edge // 2, first, second)
        else:
            value = hub_pieces[g - pairs].astype(f32)
        at = min(g, pairs)
        where = jnp.broadcast_to(home_ref[at : at + 1, :], (width, edge))
        hots[:, g * edge : (g + 1) * edge] = hot_ref[at]
        for b in range(count):
            marked[b * width : (b + 1) * width, g * edge : (g + 1) * edge] = jnp.where(
                where == b, value, 0.0
            ).astype(bf16)
    placed = lax.dot_general(
        marked[...], hots[...], (((1,), (1,)), ((), ())), preferred_element_type=f32
    )
    for b in range(count):
        cols = slice(b * span, (b + 1) * span)
        feats_ref[:, cols] = (
            back[:, cols].astype(f32) + base_ref[:, cols] + placed[b * width : (b + 1) * width]
        ).astype(bf16)


def settle(homes, hot, recv, base, lates, scale):
    width, nodes = base.shape
    domains = recv.shape[0]
    terms = (domains // 2 + 3) * edge
    return pl.pallas_call(
        functools.partial(settle_kernel, scale),
        out_shape=(
            jax.ShapeDtypeStruct((width, nodes), bf16),
            jax.ShapeDtypeStruct((width, nodes), bf16),
            jax.ShapeDtypeStruct((width, edge), f32),
            jax.ShapeDtypeStruct((width, edge), f32),
            jax.ShapeDtypeStruct((width,), f32),
        ),
        in_specs=[vmem] * (4 + len(lates)),
        out_specs=(vmem,) * 5,
        scratch_shapes=[
            pltpu.VMEM((nodes // span * width, terms), bf16),
            pltpu.VMEM((span, terms), bf16),
            pltpu.VMEM((width, nodes), bf16),
        ],
        compiler_params=params(32),
        name="settle",
    )(homes, hot, recv, base, *lates)


def swap(values, axis):
    return lax.all_to_all(values, axis, split_axis=0, concat_axis=0, tiled=True)


def trade(parts, axis):
    peers = len(parts)
    return [
        part if k == 0 else lax.ppermute(part, axis, [(i, i ^ k) for i in range(peers)])
        for k, part in enumerate(parts)
    ]


def local(
    feats,
    tile_vals,
    tile_dst,
    tile_src,
    tile_count,
    send_rows,
    hub_ids,
    w_self,
    w_neigh,
    bias,
    cotangent,
):
    nodes = feats.shape[1]
    domains = lax.axis_size("dom")
    peers = lax.axis_size("feat")
    picked, hot, homes = pick(send_rows[0], hub_ids, feats)
    picked, bias = lax.optimization_barrier((picked, bias))
    recv = swap(picked, "dom")
    parts = trade(deal(feats, cotangent, w_self, w_neigh, bias, peers), "feat")
    agg, work = gather(tile_dst, tile_src, tile_count, tile_vals, feats, recv, peers)
    agg, parts = lax.optimization_barrier((agg, parts))
    agg = swap(agg, "feat")
    near, *lates = layer(agg, parts)
    near = swap(near, "feat")
    back = away(work, near, tile_vals, domains, nodes)
    back, lates = lax.optimization_barrier((back, lates))
    back = swap(back, "dom")
    lates = trade(lates, "feat")
    base = home(work, near, tile_vals, nodes)
    scale = 1.0 / math.sqrt(nodes * domains)
    return settle(homes, hot, back, base, lates, scale)


def solution(mesh):
    placed = (
        P("feat", "dom"),
        P("dom", None, None),
        P("dom"),
        P("dom"),
        P("dom"),
        P("dom", None, None),
        P("dom"),
        P("feat", None),
        P("feat", None),
        P("feat"),
        P("feat", "dom"),
    )
    return jax.shard_map(
        local,
        mesh=mesh,
        in_specs=placed,
        out_specs=(P("feat", "dom"), P("feat", "dom"), P("feat", None), P("feat", None), P("feat")),
        check_vma=False,
    )
```

```python
import functools
import math

import jax
import jax.numpy as jnp
from jax import lax
from jax.experimental import pallas as pl
from jax.experimental.pallas import tpu as pltpu
from jax.sharding import PartitionSpec as P

edge = 128
span = 256
group = 32
kept = 64
own_blocks = 64
stride = 8
sure = 2
bf16 = jnp.bfloat16
f32 = jnp.float32
vmem = pl.BlockSpec(memory_space=pltpu.VMEM)
smem = pl.BlockSpec(memory_space=pltpu.SMEM)
hbm = pl.BlockSpec(memory_space=pl.ANY)


def params(mib):
    return pltpu.CompilerParams(vmem_limit_bytes=mib * 1024 * 1024)


def far_off(*values):
    return [pltpu.with_memory_space_constraint(value, pltpu.HBM) for value in values]


def lanes(rows):
    return lax.broadcasted_iota(jnp.int32, (rows, edge), 1)


def split(values, pieces):
    parts = []
    for _ in range(pieces):
        part = values.astype(bf16)
        parts.append(part)
        values = values - part.astype(f32)
    return parts


def column_block(column):
    hi, mid, lo = split(column, 3)
    lane = lanes(column.shape[0])
    block = jnp.where(lane == 0, hi.astype(f32), 0.0)
    block = jnp.where(lane == 1, mid.astype(f32), block)
    return jnp.where(lane == 2, lo.astype(f32), block)


def pick_kernel(
    rows_ref, hub_ref, feats_ref, out_ref, index, near, hub, wide, blocks, picked, sems
):
    width, nodes = feats_ref.shape
    count = nodes // span
    pairs = rows_ref.shape[0] // 2
    half = edge // 2
    copies = [
        pltpu.make_async_copy(feats_ref, near, sems.at[0]),
        pltpu.make_async_copy(rows_ref, wide, sems.at[1]),
        pltpu.make_async_copy(hub_ref, hub, sems.at[2]),
    ]
    for copy in copies:
        copy.start()
    copies[1].wait()
    copies[2].wait()
    lane = lanes(1)
    for g in range(pairs):
        row = jnp.concatenate([wide[2 * g : 2 * g + 1, :], wide[2 * g + 1 : 2 * g + 2, :]], axis=1)
        index[g : g + 1, :] = row
    index[pairs : pairs + 1, :] = hub[...].reshape(1, edge)
    copies[0].wait()
    for b in range(count):
        blocks[b] = near[:, b * span : (b + 1) * span]
    sub = lax.broadcasted_iota(jnp.int32, (span, edge), 0)

    def step(g, carry):
        row = index[pl.ds(g, 1), :]
        home = jnp.broadcast_to(row >> 8, (width, edge))
        hot = jnp.where(sub == (row & (span - 1)), 1.0, 0.0).astype(bf16)
        found = jnp.dot(blocks[...].reshape(count * width, span), hot, preferred_element_type=f32)
        total = found[0:width]
        for b in range(1, count):
            total = jnp.where(home == b, found[b * width : (b + 1) * width], total)
        picked[g] = total
        return carry

    lax.fori_loop(0, pairs, step, 0, unroll=16)
    step(pairs, 0)
    lane = lanes(width)
    mine = picked[pairs].astype(bf16)
    for g in range(pairs):
        here = picked[g]
        turned = pltpu.roll(here, half, 1)
        for odd in range(2):
            first, second = (turned, here) if odd else (here, turned)
            out_ref[2 * g + odd, 0:width] = mine
            out_ref[2 * g + odd, width : 2 * width] = jnp.where(lane < half, first, second).astype(
                bf16
            )


def pick(rows, hub_ids, feats):
    width, nodes = feats.shape
    domains, slots = rows.shape
    groups = domains // 2 + 1
    return pl.pallas_call(
        pick_kernel,
        out_shape=(
            jax.ShapeDtypeStruct((domains, 2 * width, edge), bf16),
            jax.ShapeDtypeStruct((groups, edge), jnp.int32),
        ),
        in_specs=[hbm, hbm, hbm],
        out_specs=(vmem, vmem),
        scratch_shapes=[
            pltpu.VMEM((width, nodes), bf16),
            pltpu.VMEM((edge,), jnp.int32),
            pltpu.VMEM((domains, slots), jnp.int32),
            pltpu.VMEM((nodes // span, width, span), bf16),
            pltpu.VMEM((groups, width, edge), f32),
            pltpu.SemaphoreType.DMA((3,)),
        ],
        compiler_params=params(32),
        name="pick",
    )(*far_off(rows, hub_ids, feats))


def deal_kernel(feats_ref, cotangent_ref, self_ref, neigh_ref, bias_ref, *rest):
    peers = len(rest) - 4
    outs, (w_self, w_neigh, bias, sems) = rest[:peers], rest[peers:]
    width, nodes = feats_ref.shape
    share = nodes // peers
    here = lax.axis_index("feat")
    small = [
        pltpu.make_async_copy(self_ref, w_self, sems.at[0]),
        pltpu.make_async_copy(neigh_ref, w_neigh, sems.at[1]),
        pltpu.make_async_copy(bias_ref, bias, sems.at[2]),
    ]
    large = []
    for k, out in enumerate(outs):
        there = pl.ds(pl.multiple_of((here ^ k) * share, share), share)
        for place, ref in enumerate((feats_ref, cotangent_ref)):
            large.append(
                pltpu.make_async_copy(
                    ref.at[:, there],
                    out.at[:, place * share : (place + 1) * share],
                    sems.at[3 + 2 * k + place],
                )
            )
    for copy in small + large:
        copy.start()
    for copy in small:
        copy.wait()
    square = (width, width)
    diagonal = lax.broadcasted_iota(jnp.int32, square, 0) == lax.broadcasted_iota(
        jnp.int32, square, 1
    )
    spread_bias = jnp.broadcast_to(bias[...].reshape(1, width), square)
    column = jnp.sum(jnp.where(diagonal, spread_bias, 0.0), axis=1, keepdims=True)
    block = column_block(column).astype(bf16)
    for out in outs:
        out[:, 2 * share : 2 * share + edge] = w_self[...]
        out[:, 2 * share + edge : 2 * share + 2 * edge] = w_neigh[...]
        out[:, 2 * share + 2 * edge : 2 * share + 3 * edge] = block
    for copy in large:
        copy.wait()


def deal(feats, cotangent, w_self, w_neigh, bias, peers):
    width, nodes = feats.shape
    part = jax.ShapeDtypeStruct((width, 2 * nodes // peers + 3 * edge), bf16)
    return pl.pallas_call(
        deal_kernel,
        out_shape=(part,) * peers,
        in_specs=[hbm] * 5,
        out_specs=(vmem,) * peers,
        scratch_shapes=[
            pltpu.VMEM((width, edge), bf16),
            pltpu.VMEM((width, edge), bf16),
            pltpu.VMEM((width,), f32),
            pltpu.SemaphoreType.DMA((3 + 2 * peers,)),
        ],
        compiler_params=params(32),
        name="deal",
    )(*far_off(feats, cotangent, w_self, w_neigh, bias))


def products_of(lefts, tiles, turned):
    results = []
    for i in range(0, len(tiles), 2):
        left = jnp.concatenate([lefts[i], lefts[i + 1]], axis=0)
        right = jnp.concatenate([tiles[i], tiles[i + 1]], axis=0 if turned else 1)
        contract = (((1,), (1 if turned else 0,)), ((), ()))
        both = lax.dot_general(left, right, contract, preferred_element_type=f32)
        width = lefts[i].shape[0]
        results += [both[:width, :edge], both[width:, edge:]]
    return results


def walk_tiles(refs, scratch, prepare, table, total, turned):
    dst_ref, src_ref, count_ref, vals_ref = refs
    dst, src, count, held, sems, tile_sems = scratch
    spare = total.shape[0] - 1
    lists = [
        pltpu.make_async_copy(count_ref, count, sems.at[0]),
        pltpu.make_async_copy(dst_ref, dst, sems.at[1]),
        pltpu.make_async_copy(src_ref, src, sems.at[2]),
    ]

    def fetch(k):
        rows = pl.ds(k * group, group)
        return pltpu.make_async_copy(vals_ref.at[rows], held.at[rows], tile_sems.at[k])

    def begin(k, carry):
        fetch(k).start()
        return carry

    for copy in lists:
        copy.start()
    for k in range(sure):
        fetch(k).start()
    prepare()
    lists[0].wait()
    live = count[0]
    groups = (live + group - 1) // group
    lax.fori_loop(sure, groups, begin, 0)
    for copy in lists[1:]:
        copy.wait()

    def some(k, carry):
        first = k * group
        lefts, places = [], []
        for i in range(group):
            t = first + i
            target, source = dst[t], src[t]
            lefts.append(table[source if turned else target])
            places.append(jnp.where(t < live, target if turned else source, spare))
        fetch(k).wait()
        tiles = [held[first + i] for i in range(group)]
        for place, product in zip(places, products_of(lefts, tiles, turned)):
            total[place] += product
        return carry

    lax.fori_loop(0, groups, some, 0)


def tile_scratch(tiles):
    return [
        pltpu.SMEM((tiles,), jnp.int32),
        pltpu.SMEM((tiles,), jnp.int32),
        pltpu.SMEM((1,), jnp.int32),
        pltpu.VMEM((tiles, edge, edge), bf16),
        pltpu.SemaphoreType.DMA((3,)),
        pltpu.SemaphoreType.DMA((tiles // group,)),
    ]


def gather_kernel(
    dst_ref, src_ref, count_ref, vals_ref, feats_ref, recv_ref, out_ref, near, table, total, sem, *scratch
):
    width, nodes = feats_ref.shape
    own = nodes // edge
    domains = recv_ref.shape[0]
    peers = out_ref.shape[0]
    features = pltpu.make_async_copy(feats_ref, near, sem)
    features.start()

    def prepare():
        lane = lanes(width)
        for g in range(domains // 2):
            table[own + g] = jnp.where(
                lane < edge // 2,
                recv_ref[2 * g, width : 2 * width].astype(f32),
                recv_ref[2 * g + 1, width : 2 * width].astype(f32),
            ).astype(bf16)
        for q in range(domains):
            table[own + domains // 2 + q] = recv_ref[q, 0:width]
        total[...] = jnp.zeros_like(total)
        features.wait()
        for b in range(own):
            table[b] = near[:, b * edge : (b + 1) * edge]

    walk_tiles((dst_ref, src_ref, count_ref, vals_ref), scratch, prepare, table, total, True)
    per = own // peers
    for b in range(own):
        col = (b % per) * edge
        out_ref[b // per, :, col : col + edge] = total[b].astype(bf16)


def gather(dst, src, count, vals, feats, recv, peers):
    width, nodes = feats.shape
    own = nodes // edge
    domains = recv.shape[0]
    return pl.pallas_call(
        gather_kernel,
        out_shape=jax.ShapeDtypeStruct((peers, width, nodes // peers), bf16),
        in_specs=[hbm] * 5 + [vmem],
        out_specs=vmem,
        scratch_shapes=[
            pltpu.VMEM((width, nodes), bf16),
            pltpu.VMEM((own + domains // 2 + domains, width, edge), bf16),
            pltpu.VMEM((own + 1, width, edge), f32),
            pltpu.SemaphoreType.DMA,
        ]
        + tile_scratch(vals.shape[0]),
        compiler_params=params(32),
        name="gather",
    )(*far_off(dst, src), count, *far_off(vals, feats), recv)


def list_kernel(
    dst_ref, src_ref, count_ref, vals_ref, work_ref, kept_ref, dst, src, count, work, sems, tile_sems
):
    copies = [
        pltpu.make_async_copy(count_ref, count, sems.at[0]),
        pltpu.make_async_copy(dst_ref, dst, sems.at[1]),
        pltpu.make_async_copy(src_ref, src, sems.at[2]),
    ]
    for copy in copies:
        copy.start()
    for copy in copies:
        copy.wait()
    tiles = dst.shape[0]
    live = count[0]

    def some(k, ends):
        low, high = ends
        for i in range(stride):
            t = k * stride + i
            source = src[t]
            alive, far = t < live, source >= own_blocks
            place = jnp.where(alive, jnp.where(far, high, low), tiles + 2)
            work[place] = t + (dst[t] << 9) + (source << 18)
            low = low + jnp.where(alive & ~far, 1, 0)
            high = high - jnp.where(alive & far, 1, 0)
        return low, high

    middle, _ = lax.fori_loop(0, (live + stride - 1) // stride, some, (0, live - 1))
    work[tiles] = middle
    work[tiles + 1] = live
    record = pltpu.make_async_copy(work, work_ref, sems.at[3])
    record.start()
    early = jnp.minimum(middle + kept, live)
    fetch(work, vals_ref, kept_ref, tile_sems, middle, early)

    def finish(k, carry):
        fetched(vals_ref, kept_ref, tile_sems, k)
        return carry

    lax.fori_loop(0, (early - middle + group - 1) // group, finish, 0)
    record.wait()


def list_tiles(dst, src, count, vals):
    tiles = dst.shape[0]
    part = jax.ShapeDtypeStruct((kept, edge, edge), bf16)
    return pl.pallas_call(
        list_kernel,
        out_shape=(jax.ShapeDtypeStruct((tiles + edge,), jnp.int32), part),
        in_specs=[hbm] * 4,
        out_specs=(vmem,) * 2,
        scratch_shapes=[
            pltpu.SMEM((tiles,), jnp.int32),
            pltpu.SMEM((tiles,), jnp.int32),
            pltpu.SMEM((1,), jnp.int32),
            pltpu.SMEM((tiles + edge,), jnp.int32),
            pltpu.SemaphoreType.DMA((4,)),
            pltpu.SemaphoreType.DMA((kept // group,)),
        ],
        compiler_params=params(16),
        name="list_tiles",
    )(*far_off(dst, src), count, *far_off(vals))


def fetch(work, vals_ref, held, sems, start, stop):
    def some(k, carry):
        for i in range(group):
            tile = work[jnp.minimum(start + k * group + i, stop - 1)] & 511
            pltpu.make_async_copy(vals_ref.at[tile], held.at[k * group + i], sems.at[k]).start()
        return carry

    lax.fori_loop(0, (stop - start + group - 1) // group, some, 0)


def fetched(vals_ref, held, sems, k):
    pltpu.make_async_copy(
        vals_ref.at[pl.ds(0, group)], held.at[pl.ds(k * group, group)], sems.at[k]
    ).wait()


def visit(work, held, ready, table, total, start, stop, turned):
    spare = total.shape[0] - 1

    def some(k, carry):
        slot = k * group
        first = start + slot
        lefts, tiles, places = [], [], []
        for i in range(group):
            code = work[jnp.minimum(first + i, stop - 1)]
            target = (code >> 9) & 511
            source = code >> 18
            lefts.append(table[source if turned else target])
            places.append(jnp.where(first + i < stop, target if turned else source, spare))
        ready(k)
        for i in range(group):
            tiles.append(held[slot + i])
        for place, product in zip(places, products_of(lefts, tiles, turned)):
            total[place] += product
        return carry

    lax.fori_loop(0, (stop - start + group - 1) // group, some, 0)


def fill_blocks(near_ref, blocks):
    own = blocks.shape[0]
    per = own // near_ref.shape[0]
    for b in range(own):
        col = (b % per) * edge
        blocks[b] = near_ref[b // per, :, col : col + edge]


def away_kernel(
    work, near_ref, kept_ref, vals_ref, out_ref, blocks, total, held, tile_sems
):
    peers, width, _ = near_ref.shape
    own = blocks.shape[0]
    share = own // peers * edge
    domains = out_ref.shape[0]
    far = own + domains // 2
    tiles = vals_ref.shape[0]
    middle, live = work[tiles], work[tiles + 1]
    early = jnp.minimum(middle + kept, live)
    fetch(work, vals_ref, held, tile_sems, early, live)
    fill_blocks(near_ref, blocks)
    total[...] = jnp.zeros_like(total)

    def summed(place):
        start = share + place * edge
        return jnp.sum(near_ref[:, :, start : start + edge].astype(f32), axis=0)

    grad_self = summed(0).astype(bf16)
    grad_neigh = summed(1).astype(bf16)
    grad_bias = column_block(jnp.sum(summed(2), axis=1, keepdims=True))
    grad_bias = pltpu.roll(grad_bias, edge // 2, 1)
    visit(work, kept_ref, lambda k: None, blocks, total, middle, early, False)
    ready = functools.partial(fetched, vals_ref, held, tile_sems)
    visit(work, held, ready, blocks, total, early, live, False)
    lane = lanes(width)
    for g in range(domains // 2):
        here = total[own + g]
        for odd in range(2):
            q = 2 * g + odd
            mine = pltpu.roll(here, edge // 2, 1) if odd else here
            out_ref[q, 0:width] = total[far + q].astype(bf16)
            out_ref[q, width : 2 * width] = jnp.where(lane < edge // 2, mine, grad_bias).astype(bf16)
            out_ref[q, 2 * width : 3 * width] = grad_self
            out_ref[q, 3 * width : 4 * width] = grad_neigh


def away(work, near, early, vals, domains, nodes):
    _, width, _ = near.shape
    tiles = vals.shape[0]
    own = nodes // edge
    return pl.pallas_call(
        away_kernel,
        out_shape=jax.ShapeDtypeStruct((domains, 4 * width, edge), bf16),
        in_specs=[smem, vmem, vmem, hbm],
        out_specs=vmem,
        scratch_shapes=[
            pltpu.VMEM((own, width, edge), bf16),
            pltpu.VMEM((own + domains // 2 + domains + 1, width, edge), f32),
            pltpu.VMEM((tiles, edge, edge), bf16),
            pltpu.SemaphoreType.DMA((tiles // group,)),
        ],
        compiler_params=params(32),
        name="away",
    )(work, near, early, *far_off(vals))


def home_kernel(work, near_ref, vals_ref, index, out_ref, hots, blocks, total, held, tile_sems):
    own = blocks.shape[0]
    tiles = vals_ref.shape[0]
    stop = work[tiles]
    fetch(work, vals_ref, held, tile_sems, 0, stop)
    fill_blocks(near_ref, blocks)
    total[...] = jnp.zeros_like(total)
    sub = lax.broadcasted_iota(jnp.int32, (span, edge), 0)
    groups = index.shape[0]
    for g in range(groups):
        hot = jnp.where(sub == (index[g : g + 1, :] & (span - 1)), 1.0, 0.0).astype(bf16)
        hots[:, g * edge : (g + 1) * edge] = hot
    for g in range(groups, groups + 2):
        hots[:, g * edge : (g + 1) * edge] = hot
    ready = functools.partial(fetched, vals_ref, held, tile_sems)
    visit(work, held, ready, blocks, total, 0, stop, False)
    for b in range(own):
        out_ref[:, b * edge : (b + 1) * edge] = total[b]


def home(work, near, vals, index, nodes):
    _, width, _ = near.shape
    tiles = vals.shape[0]
    own = nodes // edge
    return pl.pallas_call(
        home_kernel,
        out_shape=(
            jax.ShapeDtypeStruct((width, nodes), f32),
            jax.ShapeDtypeStruct((span, (index.shape[0] + 2) * edge), bf16),
        ),
        in_specs=[smem, vmem, hbm, vmem],
        out_specs=(vmem, vmem),
        scratch_shapes=[
            pltpu.VMEM((own, width, edge), bf16),
            pltpu.VMEM((own + 1, width, edge), f32),
            pltpu.VMEM((tiles, edge, edge), bf16),
            pltpu.SemaphoreType.DMA((tiles // group,)),
        ],
        compiler_params=params(32),
        name="home",
    )(work, near, *far_off(vals), index)


def layer_kernel(agg_ref, *rest):
    peers, width, share = agg_ref.shape
    rows = peers * width
    parts, near_ref, lates = rest[:peers], rest[peers], rest[peers + 1 : 2 * peers + 1]
    feats_all, cotangent_all, self_all, neigh_all, bias_all, act, back = rest[2 * peers + 1 :]
    here = lax.axis_index("feat")
    for k, part in enumerate(parts):
        peer = here ^ k
        feats_all[peer] = part[:, 0:share]
        cotangent_all[peer] = part[:, share : 2 * share]
        self_all[peer] = part[:, 2 * share : 2 * share + edge]
        neigh_all[peer] = part[:, 2 * share + edge : 2 * share + 2 * edge]
        bias_all[peer] = part[:, 2 * share + 2 * edge : 2 * share + 3 * edge]
    feats = feats_all[...].reshape(rows, share)
    cotangent = cotangent_all[...].reshape(rows, share)
    w_self = self_all[...].reshape(rows, edge)
    w_neigh = neigh_all[...].reshape(rows, edge)
    bias = jnp.sum(bias_all[...].reshape(rows, edge).astype(f32), axis=1, keepdims=True)
    aggregate = agg_ref[...].reshape(rows, share)
    first = (((0,), (0,)), ((), ()))
    last = (((1,), (1,)), ((), ()))
    linear = lax.dot_general(w_self, feats, first, preferred_element_type=f32)
    linear = linear + lax.dot_general(w_neigh, aggregate, first, preferred_element_type=f32)
    linear = linear + bias
    logistic = jax.nn.sigmoid(linear)
    act[...] = (linear * logistic).astype(bf16).reshape(peers, width, share)
    slope = logistic * (1.0 + linear * (1.0 - logistic))
    grad = (cotangent.astype(f32) * slope).astype(bf16)
    near_ref[:, :, 0:share] = (
        jnp.dot(w_neigh, grad, preferred_element_type=f32).astype(bf16).reshape(peers, width, share)
    )
    back[...] = (
        jnp.dot(w_self, grad, preferred_element_type=f32).astype(bf16).reshape(peers, width, share)
    )
    grad_self = lax.dot_general(feats, grad, last, preferred_element_type=f32)
    grad_neigh = lax.dot_general(aggregate, grad, last, preferred_element_type=f32)
    grad_bias = column_block(jnp.sum(grad.astype(f32), axis=1, keepdims=True)).astype(bf16)
    for place, piece in enumerate((grad_self.astype(bf16), grad_neigh.astype(bf16), grad_bias)):
        start = share + place * edge
        near_ref[:, :, start : start + edge] = piece.reshape(peers, width, edge)
    for k, late in enumerate(lates):
        peer = here ^ k
        late[:, 0:share] = act[peer]
        late[:, share : 2 * share] = back[peer]


def layer(agg, parts):
    peers, width, share = agg.shape
    return pl.pallas_call(
        layer_kernel,
        out_shape=(jax.ShapeDtypeStruct((peers, width, share + 3 * edge), bf16),)
        + (jax.ShapeDtypeStruct((width, 2 * share), bf16),) * peers,
        in_specs=[vmem] * (1 + peers),
        out_specs=(vmem,) * (1 + peers),
        scratch_shapes=[
            pltpu.VMEM((peers, width, share), bf16),
            pltpu.VMEM((peers, width, share), bf16),
            pltpu.VMEM((peers, width, edge), bf16),
            pltpu.VMEM((peers, width, edge), bf16),
            pltpu.VMEM((peers, width, edge), bf16),
            pltpu.VMEM((peers, width, share), bf16),
            pltpu.VMEM((peers, width, share), bf16),
        ],
        compiler_params=params(32),
        name="layer",
    )(agg, *parts)


def settle_kernel(scale, index, hots, recv_ref, base_ref, *rest):
    width, nodes = base_ref.shape
    lates, rest = rest[:-7], rest[-7:]
    act_ref, feats_ref, self_ref, neigh_ref, bias_ref, marked, back = rest
    domains = recv_ref.shape[0]
    peers = len(lates)
    share = nodes // peers
    count = nodes // span
    pairs = domains // 2
    here = lax.axis_index("feat")
    for k, late in enumerate(lates):
        peer = here ^ k
        act_ref[:, pl.ds(pl.multiple_of(peer * share, share), share)] = late[:, 0:share]
        back[:, pl.ds(pl.multiple_of(peer * share, share), share)] = late[:, share : 2 * share]
    lane = lanes(width)

    def over(start):
        return jnp.sum(recv_ref[:, start : start + width].astype(f32), axis=0)

    hub = over(0)
    self_ref[...] = over(2 * width) * scale
    neigh_ref[...] = over(3 * width) * scale
    tail = jnp.where(lane >= edge // 2, over(width), 0.0)
    column = jnp.broadcast_to(jnp.sum(tail, axis=1, keepdims=True) * scale, (width, edge))
    row = lax.broadcasted_iota(jnp.int32, (width, edge), 0)
    bias_ref[...] = jnp.sum(jnp.where(row == lane, column, 0.0), axis=0)[:width]
    hub_pieces = split(hub, 3)
    for g in range(pairs + 3):
        if g < pairs:
            first = recv_ref[2 * g, width : 2 * width].astype(f32)
            second = pltpu.roll(recv_ref[2 * g + 1, width : 2 * width].astype(f32), edge // 2, 1)
            value = jnp.where(lane < edge // 2, first, second)
        else:
            value = hub_pieces[g - pairs].astype(f32)
        at = min(g, pairs)
        where = jnp.broadcast_to(index[at : at + 1, :] >> 8, (width, edge))
        for b in range(count):
            marked[b * width : (b + 1) * width, g * edge : (g + 1) * edge] = jnp.where(
                where == b, value, 0.0
            ).astype(bf16)
    placed = lax.dot_general(
        marked[...], hots[...], (((1,), (1,)), ((), ())), preferred_element_type=f32
    )
    for b in range(count):
        cols = slice(b * span, (b + 1) * span)
        feats_ref[:, cols] = (
            back[:, cols].astype(f32) + base_ref[:, cols] + placed[b * width : (b + 1) * width]
        ).astype(bf16)


def settle(index, hots, recv, base, lates, scale):
    width, nodes = base.shape
    domains = recv.shape[0]
    terms = (domains // 2 + 3) * edge
    return pl.pallas_call(
        functools.partial(settle_kernel, scale),
        out_shape=(
            jax.ShapeDtypeStruct((width, nodes), bf16),
            jax.ShapeDtypeStruct((width, nodes), bf16),
            jax.ShapeDtypeStruct((width, edge), f32),
            jax.ShapeDtypeStruct((width, edge), f32),
            jax.ShapeDtypeStruct((width,), f32),
        ),
        in_specs=[vmem] * (4 + len(lates)),
        out_specs=(vmem,) * 5,
        scratch_shapes=[
            pltpu.VMEM((nodes // span * width, terms), bf16),
            pltpu.VMEM((width, nodes), bf16),
        ],
        compiler_params=params(32),
        name="settle",
    )(index, hots, recv, base, *lates)


def swap(values, axis):
    return lax.all_to_all(values, axis, split_axis=0, concat_axis=0, tiled=True)


def trade(parts, axis):
    peers = len(parts)
    return [
        part if k == 0 else lax.ppermute(part, axis, [(i, i ^ k) for i in range(peers)])
        for k, part in enumerate(parts)
    ]


def local(
    feats,
    tile_vals,
    tile_dst,
    tile_src,
    tile_count,
    send_rows,
    hub_ids,
    w_self,
    w_neigh,
    bias,
    cotangent,
):
    nodes = feats.shape[1]
    domains = lax.axis_size("dom")
    peers = lax.axis_size("feat")
    picked, index = pick(send_rows[0], hub_ids, feats)
    picked, bias = lax.optimization_barrier((picked, bias))
    recv = swap(picked, "dom")
    parts = trade(deal(feats, cotangent, w_self, w_neigh, bias, peers), "feat")
    agg = gather(tile_dst, tile_src, tile_count, tile_vals, feats, recv, peers)
    agg, parts = lax.optimization_barrier((agg, parts))
    agg = swap(agg, "feat")
    near, *lates = layer(agg, parts)
    near, count = lax.optimization_barrier((near, tile_count))
    near = swap(near, "feat")
    work, early = list_tiles(tile_dst, tile_src, count, tile_vals)
    back = away(work, near, early, tile_vals, domains, nodes)
    back, lates = lax.optimization_barrier((back, lates))
    back = swap(back, "dom")
    lates = trade(lates, "feat")
    base, hots = home(work, near, tile_vals, index, nodes)
    scale = 1.0 / math.sqrt(nodes * domains)
    return settle(index, hots, back, base, lates, scale)


def solution(mesh):
    placed = (
        P("feat", "dom"),
        P("dom", None, None),
        P("dom"),
        P("dom"),
        P("dom"),
        P("dom", None, None),
        P("dom"),
        P("feat", None),
        P("feat", None),
        P("feat"),
        P("feat", "dom"),
    )
    return jax.shard_map(
        local,
        mesh=mesh,
        in_specs=placed,
        out_specs=(P("feat", "dom"), P("feat", "dom"), P("feat", None), P("feat", None), P("feat")),
        check_vma=False,
    )
```

```python
import functools
import math

import jax
import jax.numpy as jnp
from jax import lax
from jax.experimental import pallas as pl
from jax.experimental.pallas import tpu as pltpu
from jax.sharding import PartitionSpec as P

edge = 128
span = 256
group = 32
sure = 2
bf16 = jnp.bfloat16
f32 = jnp.float32
vmem = pl.BlockSpec(memory_space=pltpu.VMEM)
smem = pl.BlockSpec(memory_space=pltpu.SMEM)
hbm = pl.BlockSpec(memory_space=pl.ANY)


def params(mib):
    return pltpu.CompilerParams(vmem_limit_bytes=mib * 1024 * 1024)


def far_off(*values):
    return [pltpu.with_memory_space_constraint(value, pltpu.HBM) for value in values]


def lanes(rows):
    return lax.broadcasted_iota(jnp.int32, (rows, edge), 1)


def split(values, pieces):
    parts = []
    for _ in range(pieces):
        part = values.astype(bf16)
        parts.append(part)
        values = values - part.astype(f32)
    return parts


def column_block(column):
    hi, mid, lo = split(column, 3)
    lane = lanes(column.shape[0])
    block = jnp.where(lane == 0, hi.astype(f32), 0.0)
    block = jnp.where(lane == 1, mid.astype(f32), block)
    return jnp.where(lane == 2, lo.astype(f32), block)


def start_all(pairs, sems):
    copies = []
    for place, (source, target) in enumerate(pairs):
        copies.append(pltpu.make_async_copy(source, target, sems.at[place]))
        copies[-1].start()
    return copies


def pick_kernel(
    rows_ref,
    hub_ref,
    feats_ref,
    cotangent_ref,
    self_ref,
    neigh_ref,
    bias_ref,
    dst_ref,
    src_ref,
    count_ref,
    out_ref,
    index,
    work_ref,
    *rest,
):
    parts, rest = rest[:-14], rest[-14:]
    near, hub, wide, blocks, picked, w_self, w_neigh, bias, dst, src, count, work, sems, part_sems = rest
    width, nodes = feats_ref.shape
    span_count = nodes // span
    own = nodes // edge
    pairs = rows_ref.shape[0] // 2
    peers = len(parts)
    share = nodes // peers
    half = edge // 2
    tiles = dst.shape[0]
    per_step = tiles // pairs
    copies = start_all(
        (
            (count_ref, count),
            (rows_ref, wide),
            (hub_ref, hub),
            (feats_ref, near),
            (dst_ref, dst),
            (src_ref, src),
            (self_ref, w_self),
            (neigh_ref, w_neigh),
            (bias_ref, bias),
        ),
        sems,
    )
    here = lax.axis_index("feat")
    moves = []
    for k, part in enumerate(parts):
        there = pl.ds(pl.multiple_of((here ^ k) * share, share), share)
        moves.append((feats_ref.at[:, there], part.at[:, 0:share]))
        moves.append((cotangent_ref.at[:, there], part.at[:, share : 2 * share]))
    moves = start_all(moves, part_sems)
    for copy in copies[:3]:
        copy.wait()
    for g in range(pairs):
        row = jnp.concatenate([wide[2 * g : 2 * g + 1, :], wide[2 * g + 1 : 2 * g + 2, :]], axis=1)
        index[g : g + 1, :] = row
    index[pairs : pairs + 1, :] = hub[...].reshape(1, edge)
    for copy in copies[3:]:
        copy.wait()
    live = count[0]
    for b in range(span_count):
        blocks[b] = near[:, b * span : (b + 1) * span]
    sub = lax.broadcasted_iota(jnp.int32, (span, edge), 0)

    def find(g):
        row = index[pl.ds(g, 1), :]
        home = jnp.broadcast_to(row >> 8, (width, edge))
        hot = jnp.where(sub == (row & (span - 1)), 1.0, 0.0).astype(bf16)
        whole = blocks[...].reshape(span_count * width, span)
        found = jnp.dot(whole, hot, preferred_element_type=f32)
        total = found[0:width]
        for b in range(1, span_count):
            total = jnp.where(home == b, found[b * width : (b + 1) * width], total)
        picked[g] = total

    def step(g, ends):
        low, high = ends
        find(g)
        for i in range(per_step):
            t = g * per_step + i
            source = src[t]
            alive, far = t < live, source >= own
            place = jnp.where(alive, jnp.where(far, high, low), tiles + 2)
            work[place] = t + (dst[t] << 9) + (source << 18)
            low = low + jnp.where(alive & ~far, 1, 0)
            high = high - jnp.where(alive & far, 1, 0)
        return low, high

    middle, _ = lax.fori_loop(0, pairs, step, (0, live - 1), unroll=pairs)
    work[tiles] = middle
    work[tiles + 1] = live
    record = pltpu.make_async_copy(work, work_ref, sems.at[9])
    record.start()
    find(pairs)
    lane = lanes(width)
    mine = picked[pairs].astype(bf16)
    for g in range(pairs):
        here = picked[g]
        turned = pltpu.roll(here, half, 1)
        for odd in range(2):
            first, second = (turned, here) if odd else (here, turned)
            out_ref[2 * g + odd, 0:width] = mine
            out_ref[2 * g + odd, width : 2 * width] = jnp.where(lane < half, first, second).astype(
                bf16
            )
    square = (width, width)
    diagonal = lax.broadcasted_iota(jnp.int32, square, 0) == lax.broadcasted_iota(
        jnp.int32, square, 1
    )
    spread_bias = jnp.broadcast_to(bias[...].reshape(1, width), square)
    column = jnp.sum(jnp.where(diagonal, spread_bias, 0.0), axis=1, keepdims=True)
    block = column_block(column).astype(bf16)
    for part in parts:
        part[:, 2 * share : 2 * share + edge] = w_self[...]
        part[:, 2 * share + edge : 2 * share + 2 * edge] = w_neigh[...]
        part[:, 2 * share + 2 * edge : 2 * share + 3 * edge] = block
    for move in moves:
        move.wait()
    record.wait()


def pick(rows, hub_ids, feats, cotangent, w_self, w_neigh, bias, dst, src, count, peers):
    width, nodes = feats.shape
    domains, slots = rows.shape
    groups = domains // 2 + 1
    tiles = dst.shape[0]
    part = jax.ShapeDtypeStruct((width, 2 * nodes // peers + 3 * edge), bf16)
    return pl.pallas_call(
        pick_kernel,
        out_shape=(
            jax.ShapeDtypeStruct((domains, 2 * width, edge), bf16),
            jax.ShapeDtypeStruct((groups, edge), jnp.int32),
            jax.ShapeDtypeStruct((tiles + edge,), jnp.int32),
        )
        + (part,) * peers,
        in_specs=[hbm] * 10,
        out_specs=(vmem,) * (3 + peers),
        scratch_shapes=[
            pltpu.VMEM((width, nodes), bf16),
            pltpu.VMEM((edge,), jnp.int32),
            pltpu.VMEM((domains, slots), jnp.int32),
            pltpu.VMEM((nodes // span, width, span), bf16),
            pltpu.VMEM((groups, width, edge), f32),
            pltpu.VMEM((width, edge), bf16),
            pltpu.VMEM((width, edge), bf16),
            pltpu.VMEM((width,), f32),
            pltpu.SMEM((tiles,), jnp.int32),
            pltpu.SMEM((tiles,), jnp.int32),
            pltpu.SMEM((1,), jnp.int32),
            pltpu.SMEM((tiles + edge,), jnp.int32),
            pltpu.SemaphoreType.DMA((10,)),
            pltpu.SemaphoreType.DMA((2 * peers,)),
        ],
        compiler_params=params(32),
        name="pick",
    )(
        *far_off(rows, hub_ids, feats, cotangent, w_self, w_neigh, bias, dst, src),
        count,
    )


def products_of(lefts, tiles, turned):
    results = []
    for i in range(0, len(tiles), 2):
        left = jnp.concatenate([lefts[i], lefts[i + 1]], axis=0)
        right = jnp.concatenate([tiles[i], tiles[i + 1]], axis=0 if turned else 1)
        contract = (((1,), (1 if turned else 0,)), ((), ()))
        both = lax.dot_general(left, right, contract, preferred_element_type=f32)
        width = lefts[i].shape[0]
        results += [both[:width, :edge], both[width:, edge:]]
    return results


def walk_tiles(refs, scratch, prepare, table, total, turned):
    dst_ref, src_ref, count_ref, vals_ref = refs
    dst, src, count, held, sems, tile_sems = scratch
    spare = total.shape[0] - 1
    lists = [
        pltpu.make_async_copy(count_ref, count, sems.at[0]),
        pltpu.make_async_copy(dst_ref, dst, sems.at[1]),
        pltpu.make_async_copy(src_ref, src, sems.at[2]),
    ]

    def fetch(k):
        rows = pl.ds(k * group, group)
        return pltpu.make_async_copy(vals_ref.at[rows], held.at[rows], tile_sems.at[k])

    def begin(k, carry):
        fetch(k).start()
        return carry

    for copy in lists:
        copy.start()
    for k in range(sure):
        fetch(k).start()
    prepare()
    lists[0].wait()
    live = count[0]
    groups = (live + group - 1) // group
    lax.fori_loop(sure, groups, begin, 0)
    for copy in lists[1:]:
        copy.wait()

    def some(k, carry):
        first = k * group
        lefts, places = [], []
        for i in range(group):
            t = first + i
            target, source = dst[t], src[t]
            lefts.append(table[source if turned else target])
            places.append(jnp.where(t < live, target if turned else source, spare))
        fetch(k).wait()
        tiles = [held[first + i] for i in range(group)]
        for place, product in zip(places, products_of(lefts, tiles, turned)):
            total[place] += product
        return carry

    lax.fori_loop(0, groups, some, 0)


def tile_scratch(tiles):
    return [
        pltpu.SMEM((tiles,), jnp.int32),
        pltpu.SMEM((tiles,), jnp.int32),
        pltpu.SMEM((1,), jnp.int32),
        pltpu.VMEM((tiles, edge, edge), bf16),
        pltpu.SemaphoreType.DMA((3,)),
        pltpu.SemaphoreType.DMA((tiles // group,)),
    ]


def gather_kernel(
    dst_ref, src_ref, count_ref, vals_ref, feats_ref, recv_ref, out_ref, near, table, total, sem, *scratch
):
    width, nodes = feats_ref.shape
    own = nodes // edge
    domains = recv_ref.shape[0]
    peers = out_ref.shape[0]
    features = pltpu.make_async_copy(feats_ref, near, sem)
    features.start()

    def prepare():
        lane = lanes(width)
        for g in range(domains // 2):
            table[own + g] = jnp.where(
                lane < edge // 2,
                recv_ref[2 * g, width : 2 * width].astype(f32),
                recv_ref[2 * g + 1, width : 2 * width].astype(f32),
            ).astype(bf16)
        for q in range(domains):
            table[own + domains // 2 + q] = recv_ref[q, 0:width]
        total[...] = jnp.zeros_like(total)
        features.wait()
        for b in range(own):
            table[b] = near[:, b * edge : (b + 1) * edge]

    walk_tiles((dst_ref, src_ref, count_ref, vals_ref), scratch, prepare, table, total, True)
    per = own // peers
    for b in range(own):
        col = (b % per) * edge
        out_ref[b // per, :, col : col + edge] = total[b].astype(bf16)


def gather(dst, src, count, vals, feats, recv, peers):
    width, nodes = feats.shape
    own = nodes // edge
    domains = recv.shape[0]
    return pl.pallas_call(
        gather_kernel,
        out_shape=jax.ShapeDtypeStruct((peers, width, nodes // peers), bf16),
        in_specs=[hbm] * 5 + [vmem],
        out_specs=vmem,
        scratch_shapes=[
            pltpu.VMEM((width, nodes), bf16),
            pltpu.VMEM((own + domains // 2 + domains, width, edge), bf16),
            pltpu.VMEM((own + 1, width, edge), f32),
            pltpu.SemaphoreType.DMA,
        ]
        + tile_scratch(vals.shape[0]),
        compiler_params=params(32),
        name="gather",
    )(*far_off(dst, src), count, *far_off(vals, feats), recv)


def fetch(work, vals_ref, held, sems, start, stop):
    def some(k, carry):
        for i in range(group):
            tile = work[jnp.minimum(start + k * group + i, stop - 1)] & 511
            pltpu.make_async_copy(vals_ref.at[tile], held.at[k * group + i], sems.at[k]).start()
        return carry

    lax.fori_loop(0, (stop - start + group - 1) // group, some, 0)


def fetched(vals_ref, held, sems, k):
    pltpu.make_async_copy(
        vals_ref.at[pl.ds(0, group)], held.at[pl.ds(k * group, group)], sems.at[k]
    ).wait()


def visit(work, held, ready, table, total, start, stop, turned):
    spare = total.shape[0] - 1

    def some(k, carry):
        slot = k * group
        first = start + slot
        lefts, tiles, places = [], [], []
        for i in range(group):
            code = work[jnp.minimum(first + i, stop - 1)]
            target = (code >> 9) & 511
            source = code >> 18
            lefts.append(table[source if turned else target])
            places.append(jnp.where(first + i < stop, target if turned else source, spare))
        ready(k)
        for i in range(group):
            tiles.append(held[slot + i])
        for place, product in zip(places, products_of(lefts, tiles, turned)):
            total[place] += product
        return carry

    lax.fori_loop(0, (stop - start + group - 1) // group, some, 0)


def fill_blocks(near_ref, blocks):
    own = blocks.shape[0]
    per = own // near_ref.shape[0]
    for b in range(own):
        col = (b % per) * edge
        blocks[b] = near_ref[b // per, :, col : col + edge]


def away_kernel(
    work, near_ref, vals_ref, out_ref, blocks, total, held, tile_sems
):
    peers, width, _ = near_ref.shape
    own = blocks.shape[0]
    share = own // peers * edge
    domains = out_ref.shape[0]
    far = own + domains // 2
    tiles = vals_ref.shape[0]
    middle, live = work[tiles], work[tiles + 1]
    fetch(work, vals_ref, held, tile_sems, middle, live)
    fill_blocks(near_ref, blocks)
    total[...] = jnp.zeros_like(total)

    def summed(place):
        start = share + place * edge
        return jnp.sum(near_ref[:, :, start : start + edge].astype(f32), axis=0)

    grad_self = summed(0).astype(bf16)
    grad_neigh = summed(1).astype(bf16)
    grad_bias = column_block(jnp.sum(summed(2), axis=1, keepdims=True))
    grad_bias = pltpu.roll(grad_bias, edge // 2, 1)
    ready = functools.partial(fetched, vals_ref, held, tile_sems)
    visit(work, held, ready, blocks, total, middle, live, False)
    lane = lanes(width)
    for g in range(domains // 2):
        here = total[own + g]
        for odd in range(2):
            q = 2 * g + odd
            mine = pltpu.roll(here, edge // 2, 1) if odd else here
            out_ref[q, 0:width] = total[far + q].astype(bf16)
            out_ref[q, width : 2 * width] = jnp.where(lane < edge // 2, mine, grad_bias).astype(bf16)
            out_ref[q, 2 * width : 3 * width] = grad_self
            out_ref[q, 3 * width : 4 * width] = grad_neigh


def away(work, near, vals, domains, nodes):
    _, width, _ = near.shape
    tiles = vals.shape[0]
    own = nodes // edge
    return pl.pallas_call(
        away_kernel,
        out_shape=jax.ShapeDtypeStruct((domains, 4 * width, edge), bf16),
        in_specs=[smem, vmem, hbm],
        out_specs=vmem,
        scratch_shapes=[
            pltpu.VMEM((own, width, edge), bf16),
            pltpu.VMEM((own + domains // 2 + domains + 1, width, edge), f32),
            pltpu.VMEM((tiles, edge, edge), bf16),
            pltpu.SemaphoreType.DMA((tiles // group,)),
        ],
        compiler_params=params(32),
        name="away",
    )(work, near, *far_off(vals))


def home_kernel(work, near_ref, vals_ref, index, out_ref, hots, blocks, total, held, tile_sems):
    own = blocks.shape[0]
    tiles = vals_ref.shape[0]
    stop = work[tiles]
    fetch(work, vals_ref, held, tile_sems, 0, stop)
    fill_blocks(near_ref, blocks)
    total[...] = jnp.zeros_like(total)
    sub = lax.broadcasted_iota(jnp.int32, (span, edge), 0)
    groups = index.shape[0]
    for g in range(groups):
        hot = jnp.where(sub == (index[g : g + 1, :] & (span - 1)), 1.0, 0.0).astype(bf16)
        hots[:, g * edge : (g + 1) * edge] = hot
    for g in range(groups, groups + 2):
        hots[:, g * edge : (g + 1) * edge] = hot
    ready = functools.partial(fetched, vals_ref, held, tile_sems)
    visit(work, held, ready, blocks, total, 0, stop, False)
    for b in range(own):
        out_ref[:, b * edge : (b + 1) * edge] = total[b]


def home(work, near, vals, index, nodes):
    _, width, _ = near.shape
    tiles = vals.shape[0]
    own = nodes // edge
    return pl.pallas_call(
        home_kernel,
        out_shape=(
            jax.ShapeDtypeStruct((width, nodes), f32),
            jax.ShapeDtypeStruct((span, (index.shape[0] + 2) * edge), bf16),
        ),
        in_specs=[smem, vmem, hbm, vmem],
        out_specs=(vmem, vmem),
        scratch_shapes=[
            pltpu.VMEM((own, width, edge), bf16),
            pltpu.VMEM((own + 1, width, edge), f32),
            pltpu.VMEM((tiles, edge, edge), bf16),
            pltpu.SemaphoreType.DMA((tiles // group,)),
        ],
        compiler_params=params(32),
        name="home",
    )(work, near, *far_off(vals), index)


def layer_kernel(agg_ref, *rest):
    peers, width, share = agg_ref.shape
    rows = peers * width
    parts, near_ref, lates = rest[:peers], rest[peers], rest[peers + 1 : 2 * peers + 1]
    feats_all, cotangent_all, self_all, neigh_all, bias_all, act, back = rest[2 * peers + 1 :]
    here = lax.axis_index("feat")
    for k, part in enumerate(parts):
        peer = here ^ k
        feats_all[peer] = part[:, 0:share]
        cotangent_all[peer] = part[:, share : 2 * share]
        self_all[peer] = part[:, 2 * share : 2 * share + edge]
        neigh_all[peer] = part[:, 2 * share + edge : 2 * share + 2 * edge]
        bias_all[peer] = part[:, 2 * share + 2 * edge : 2 * share + 3 * edge]
    feats = feats_all[...].reshape(rows, share)
    cotangent = cotangent_all[...].reshape(rows, share)
    w_self = self_all[...].reshape(rows, edge)
    w_neigh = neigh_all[...].reshape(rows, edge)
    bias = jnp.sum(bias_all[...].reshape(rows, edge).astype(f32), axis=1, keepdims=True)
    aggregate = agg_ref[...].reshape(rows, share)
    first = (((0,), (0,)), ((), ()))
    last = (((1,), (1,)), ((), ()))
    linear = lax.dot_general(w_self, feats, first, preferred_element_type=f32)
    linear = linear + lax.dot_general(w_neigh, aggregate, first, preferred_element_type=f32)
    linear = linear + bias
    logistic = jax.nn.sigmoid(linear)
    act[...] = (linear * logistic).astype(bf16).reshape(peers, width, share)
    slope = logistic * (1.0 + linear * (1.0 - logistic))
    grad = (cotangent.astype(f32) * slope).astype(bf16)
    near_ref[:, :, 0:share] = (
        jnp.dot(w_neigh, grad, preferred_element_type=f32).astype(bf16).reshape(peers, width, share)
    )
    back[...] = (
        jnp.dot(w_self, grad, preferred_element_type=f32).astype(bf16).reshape(peers, width, share)
    )
    grad_self = lax.dot_general(feats, grad, last, preferred_element_type=f32)
    grad_neigh = lax.dot_general(aggregate, grad, last, preferred_element_type=f32)
    grad_bias = column_block(jnp.sum(grad.astype(f32), axis=1, keepdims=True)).astype(bf16)
    for place, piece in enumerate((grad_self.astype(bf16), grad_neigh.astype(bf16), grad_bias)):
        start = share + place * edge
        near_ref[:, :, start : start + edge] = piece.reshape(peers, width, edge)
    for k, late in enumerate(lates):
        peer = here ^ k
        late[:, 0:share] = act[peer]
        late[:, share : 2 * share] = back[peer]


def layer(agg, parts):
    peers, width, share = agg.shape
    return pl.pallas_call(
        layer_kernel,
        out_shape=(jax.ShapeDtypeStruct((peers, width, share + 3 * edge), bf16),)
        + (jax.ShapeDtypeStruct((width, 2 * share), bf16),) * peers,
        in_specs=[vmem] * (1 + peers),
        out_specs=(vmem,) * (1 + peers),
        scratch_shapes=[
            pltpu.VMEM((peers, width, share), bf16),
            pltpu.VMEM((peers, width, share), bf16),
            pltpu.VMEM((peers, width, edge), bf16),
            pltpu.VMEM((peers, width, edge), bf16),
            pltpu.VMEM((peers, width, edge), bf16),
            pltpu.VMEM((peers, width, share), bf16),
            pltpu.VMEM((peers, width, share), bf16),
        ],
        compiler_params=params(32),
        name="layer",
    )(agg, *parts)


def settle_kernel(scale, index, hots, recv_ref, base_ref, *rest):
    width, nodes = base_ref.shape
    lates, rest = rest[:-7], rest[-7:]
    act_ref, feats_ref, self_ref, neigh_ref, bias_ref, marked, back = rest
    domains = recv_ref.shape[0]
    peers = len(lates)
    share = nodes // peers
    count = nodes // span
    pairs = domains // 2
    here = lax.axis_index("feat")
    for k, late in enumerate(lates):
        peer = here ^ k
        act_ref[:, pl.ds(pl.multiple_of(peer * share, share), share)] = late[:, 0:share]
        back[:, pl.ds(pl.multiple_of(peer * share, share), share)] = late[:, share : 2 * share]
    lane = lanes(width)

    def over(start):
        return jnp.sum(recv_ref[:, start : start + width].astype(f32), axis=0)

    hub = over(0)
    self_ref[...] = over(2 * width) * scale
    neigh_ref[...] = over(3 * width) * scale
    tail = jnp.where(lane >= edge // 2, over(width), 0.0)
    column = jnp.broadcast_to(jnp.sum(tail, axis=1, keepdims=True) * scale, (width, edge))
    row = lax.broadcasted_iota(jnp.int32, (width, edge), 0)
    bias_ref[...] = jnp.sum(jnp.where(row == lane, column, 0.0), axis=0)[:width]
    hub_pieces = split(hub, 3)
    for g in range(pairs + 3):
        if g < pairs:
            first = recv_ref[2 * g, width : 2 * width].astype(f32)
            second = pltpu.roll(recv_ref[2 * g + 1, width : 2 * width].astype(f32), edge // 2, 1)
            value = jnp.where(lane < edge // 2, first, second)
        else:
            value = hub_pieces[g - pairs].astype(f32)
        at = min(g, pairs)
        where = jnp.broadcast_to(index[at : at + 1, :] >> 8, (width, edge))
        for b in range(count):
            marked[b * width : (b + 1) * width, g * edge : (g + 1) * edge] = jnp.where(
                where == b, value, 0.0
            ).astype(bf16)
    placed = lax.dot_general(
        marked[...], hots[...], (((1,), (1,)), ((), ())), preferred_element_type=f32
    )
    for b in range(count):
        cols = slice(b * span, (b + 1) * span)
        feats_ref[:, cols] = (
            back[:, cols].astype(f32) + base_ref[:, cols] + placed[b * width : (b + 1) * width]
        ).astype(bf16)


def settle(index, hots, recv, base, lates, scale):
    width, nodes = base.shape
    domains = recv.shape[0]
    terms = (domains // 2 + 3) * edge
    return pl.pallas_call(
        functools.partial(settle_kernel, scale),
        out_shape=(
            jax.ShapeDtypeStruct((width, nodes), bf16),
            jax.ShapeDtypeStruct((width, nodes), bf16),
            jax.ShapeDtypeStruct((width, edge), f32),
            jax.ShapeDtypeStruct((width, edge), f32),
            jax.ShapeDtypeStruct((width,), f32),
        ),
        in_specs=[vmem] * (4 + len(lates)),
        out_specs=(vmem,) * 5,
        scratch_shapes=[
            pltpu.VMEM((nodes // span * width, terms), bf16),
            pltpu.VMEM((width, nodes), bf16),
        ],
        compiler_params=params(32),
        name="settle",
    )(index, hots, recv, base, *lates)


def swap(values, axis):
    return lax.all_to_all(values, axis, split_axis=0, concat_axis=0, tiled=True)


def trade(parts, axis):
    peers = len(parts)
    return [
        part if k == 0 else lax.ppermute(part, axis, [(i, i ^ k) for i in range(peers)])
        for k, part in enumerate(parts)
    ]


def local(
    feats,
    tile_vals,
    tile_dst,
    tile_src,
    tile_count,
    send_rows,
    hub_ids,
    w_self,
    w_neigh,
    bias,
    cotangent,
):
    nodes = feats.shape[1]
    domains = lax.axis_size("dom")
    peers = lax.axis_size("feat")
    picked, index, work, *parts = pick(
        send_rows[0],
        hub_ids,
        feats,
        cotangent,
        w_self,
        w_neigh,
        bias,
        tile_dst,
        tile_src,
        tile_count,
        peers,
    )
    recv = swap(picked, "dom")
    parts = trade(parts, "feat")
    agg = gather(tile_dst, tile_src, tile_count, tile_vals, feats, recv, peers)
    agg, parts = lax.optimization_barrier((agg, parts))
    agg = swap(agg, "feat")
    near, *lates = layer(agg, parts)
    near = swap(near, "feat")
    back = away(work, near, tile_vals, domains, nodes)
    back, lates = lax.optimization_barrier((back, lates))
    back = swap(back, "dom")
    lates = trade(lates, "feat")
    base, hots = home(work, near, tile_vals, index, nodes)
    scale = 1.0 / math.sqrt(nodes * domains)
    return settle(index, hots, back, base, lates, scale)


def solution(mesh):
    placed = (
        P("feat", "dom"),
        P("dom", None, None),
        P("dom"),
        P("dom"),
        P("dom"),
        P("dom", None, None),
        P("dom"),
        P("feat", None),
        P("feat", None),
        P("feat"),
        P("feat", "dom"),
    )
    return jax.shard_map(
        local,
        mesh=mesh,
        in_specs=placed,
        out_specs=(P("feat", "dom"), P("feat", "dom"), P("feat", None), P("feat", None), P("feat")),
        check_vma=False,
    )
```

```python
import functools
import math

import jax
import jax.numpy as jnp
from jax import lax
from jax.experimental import pallas as pl
from jax.experimental.pallas import tpu as pltpu
from jax.sharding import PartitionSpec as P

edge = 128
span = 256
group = 32
sure = 2
bf16 = jnp.bfloat16
f32 = jnp.float32
vmem = pl.BlockSpec(memory_space=pltpu.VMEM)
smem = pl.BlockSpec(memory_space=pltpu.SMEM)
hbm = pl.BlockSpec(memory_space=pl.ANY)


def params(mib):
    return pltpu.CompilerParams(vmem_limit_bytes=mib * 1024 * 1024)


def far_off(*values):
    return [pltpu.with_memory_space_constraint(value, pltpu.HBM) for value in values]


def lanes(rows):
    return lax.broadcasted_iota(jnp.int32, (rows, edge), 1)


def split(values, pieces):
    parts = []
    for _ in range(pieces):
        part = values.astype(bf16)
        parts.append(part)
        values = values - part.astype(f32)
    return parts


def column_block(column):
    hi, mid, lo = split(column, 3)
    lane = lanes(column.shape[0])
    block = jnp.where(lane == 0, hi.astype(f32), 0.0)
    block = jnp.where(lane == 1, mid.astype(f32), block)
    return jnp.where(lane == 2, lo.astype(f32), block)


def start_all(pairs, sems):
    copies = []
    for place, (source, target) in enumerate(pairs):
        copies.append(pltpu.make_async_copy(source, target, sems.at[place]))
        copies[-1].start()
    return copies


def pick_kernel(
    rows_ref,
    hub_ref,
    feats_ref,
    cotangent_ref,
    self_ref,
    neigh_ref,
    bias_ref,
    out_ref,
    index,
    *rest,
):
    parts, rest = rest[:-10], rest[-10:]
    near, hub, wide, blocks, picked, w_self, w_neigh, bias, sems, part_sems = rest
    width, nodes = feats_ref.shape
    span_count = nodes // span
    pairs = rows_ref.shape[0] // 2
    peers = len(parts)
    share = nodes // peers
    half = edge // 2
    copies = start_all(
        (
            (rows_ref, wide),
            (hub_ref, hub),
            (feats_ref, near),
            (self_ref, w_self),
            (neigh_ref, w_neigh),
            (bias_ref, bias),
        ),
        sems,
    )
    here = lax.axis_index("feat")
    moves = []
    for k, part in enumerate(parts):
        there = pl.ds(pl.multiple_of((here ^ k) * share, share), share)
        moves.append((feats_ref.at[:, there], part.at[:, 0:share]))
        moves.append((cotangent_ref.at[:, there], part.at[:, share : 2 * share]))
    moves = start_all(moves, part_sems)
    for copy in copies[:2]:
        copy.wait()
    for g in range(pairs):
        row = jnp.concatenate([wide[2 * g : 2 * g + 1, :], wide[2 * g + 1 : 2 * g + 2, :]], axis=1)
        index[g : g + 1, :] = row
    index[pairs : pairs + 1, :] = hub[...].reshape(1, edge)
    for copy in copies[2:]:
        copy.wait()
    for b in range(span_count):
        blocks[b] = near[:, b * span : (b + 1) * span]
    sub = lax.broadcasted_iota(jnp.int32, (span, edge), 0)

    def find(g, carry):
        row = index[pl.ds(g, 1), :]
        home = jnp.broadcast_to(row >> 8, (width, edge))
        hot = jnp.where(sub == (row & (span - 1)), 1.0, 0.0).astype(bf16)
        whole = blocks[...].reshape(span_count * width, span)
        found = jnp.dot(whole, hot, preferred_element_type=f32)
        total = found[0:width]
        for b in range(1, span_count):
            total = jnp.where(home == b, found[b * width : (b + 1) * width], total)
        picked[g] = total
        return carry

    lax.fori_loop(0, pairs, find, 0, unroll=pairs)
    find(pairs, 0)
    lane = lanes(width)
    mine = picked[pairs].astype(bf16)
    for g in range(pairs):
        here = picked[g]
        turned = pltpu.roll(here, half, 1)
        for odd in range(2):
            first, second = (turned, here) if odd else (here, turned)
            out_ref[2 * g + odd, 0:width] = mine
            out_ref[2 * g + odd, width : 2 * width] = jnp.where(lane < half, first, second).astype(
                bf16
            )
    square = (width, width)
    diagonal = lax.broadcasted_iota(jnp.int32, square, 0) == lax.broadcasted_iota(
        jnp.int32, square, 1
    )
    spread_bias = jnp.broadcast_to(bias[...].reshape(1, width), square)
    column = jnp.sum(jnp.where(diagonal, spread_bias, 0.0), axis=1, keepdims=True)
    block = column_block(column).astype(bf16)
    for part in parts:
        part[:, 2 * share : 2 * share + edge] = w_self[...]
        part[:, 2 * share + edge : 2 * share + 2 * edge] = w_neigh[...]
        part[:, 2 * share + 2 * edge : 2 * share + 3 * edge] = block
    for move in moves:
        move.wait()


def pick(rows, hub_ids, feats, cotangent, w_self, w_neigh, bias, peers):
    width, nodes = feats.shape
    domains, slots = rows.shape
    groups = domains // 2 + 1
    part = jax.ShapeDtypeStruct((width, 2 * nodes // peers + 3 * edge), bf16)
    return pl.pallas_call(
        pick_kernel,
        out_shape=(
            jax.ShapeDtypeStruct((domains, 2 * width, edge), bf16),
            jax.ShapeDtypeStruct((groups, edge), jnp.int32),
        )
        + (part,) * peers,
        in_specs=[hbm] * 7,
        out_specs=(vmem,) * (2 + peers),
        scratch_shapes=[
            pltpu.VMEM((width, nodes), bf16),
            pltpu.VMEM((edge,), jnp.int32),
            pltpu.VMEM((domains, slots), jnp.int32),
            pltpu.VMEM((nodes // span, width, span), bf16),
            pltpu.VMEM((groups, width, edge), f32),
            pltpu.VMEM((width, edge), bf16),
            pltpu.VMEM((width, edge), bf16),
            pltpu.VMEM((width,), f32),
            pltpu.SemaphoreType.DMA((7,)),
            pltpu.SemaphoreType.DMA((2 * peers,)),
        ],
        compiler_params=params(32),
        name="pick",
    )(*far_off(rows, hub_ids, feats, cotangent, w_self, w_neigh, bias))


def products_of(lefts, tiles, turned):
    results = []
    for i in range(0, len(tiles), 2):
        left = jnp.concatenate([lefts[i], lefts[i + 1]], axis=0)
        right = jnp.concatenate([tiles[i], tiles[i + 1]], axis=0 if turned else 1)
        contract = (((1,), (1 if turned else 0,)), ((), ()))
        both = lax.dot_general(left, right, contract, preferred_element_type=f32)
        width = lefts[i].shape[0]
        results += [both[:width, :edge], both[width:, edge:]]
    return results


def walk_tiles(refs, scratch, prepare, table, total, turned):
    dst_ref, src_ref, count_ref, vals_ref = refs
    dst, src, count, held, sems, tile_sems = scratch
    spare = total.shape[0] - 1
    lists = [
        pltpu.make_async_copy(count_ref, count, sems.at[0]),
        pltpu.make_async_copy(dst_ref, dst, sems.at[1]),
        pltpu.make_async_copy(src_ref, src, sems.at[2]),
    ]

    def fetch(k):
        rows = pl.ds(k * group, group)
        return pltpu.make_async_copy(vals_ref.at[rows], held.at[rows], tile_sems.at[k])

    def begin(k, carry):
        fetch(k).start()
        return carry

    for copy in lists:
        copy.start()
    for k in range(sure):
        fetch(k).start()
    prepare()
    lists[0].wait()
    live = count[0]
    groups = (live + group - 1) // group
    lax.fori_loop(sure, groups, begin, 0)
    for copy in lists[1:]:
        copy.wait()

    def some(k, carry):
        first = k * group
        lefts, places = [], []
        for i in range(group):
            t = first + i
            target, source = dst[t], src[t]
            lefts.append(table[source if turned else target])
            places.append(jnp.where(t < live, target if turned else source, spare))
        fetch(k).wait()
        tiles = [held[first + i] for i in range(group)]
        for place, product in zip(places, products_of(lefts, tiles, turned)):
            total[place] += product
        return carry

    lax.fori_loop(0, groups, some, 0)


def tile_scratch(tiles):
    return [
        pltpu.SMEM((tiles,), jnp.int32),
        pltpu.SMEM((tiles,), jnp.int32),
        pltpu.SMEM((1,), jnp.int32),
        pltpu.VMEM((tiles, edge, edge), bf16),
        pltpu.SemaphoreType.DMA((3,)),
        pltpu.SemaphoreType.DMA((tiles // group,)),
    ]


def gather_kernel(
    dst_ref, src_ref, count_ref, vals_ref, feats_ref, recv_ref, out_ref, near, table, total, sem, *scratch
):
    width, nodes = feats_ref.shape
    own = nodes // edge
    domains = recv_ref.shape[0]
    peers = out_ref.shape[0]
    features = pltpu.make_async_copy(feats_ref, near, sem)
    features.start()

    def prepare():
        lane = lanes(width)
        for g in range(domains // 2):
            table[own + g] = jnp.where(
                lane < edge // 2,
                recv_ref[2 * g, width : 2 * width].astype(f32),
                recv_ref[2 * g + 1, width : 2 * width].astype(f32),
            ).astype(bf16)
        for q in range(domains):
            table[own + domains // 2 + q] = recv_ref[q, 0:width]
        total[...] = jnp.zeros_like(total)
        features.wait()
        for b in range(own):
            table[b] = near[:, b * edge : (b + 1) * edge]

    walk_tiles((dst_ref, src_ref, count_ref, vals_ref), scratch, prepare, table, total, True)
    per = own // peers
    for b in range(own):
        col = (b % per) * edge
        out_ref[b // per, :, col : col + edge] = total[b].astype(bf16)


def gather(dst, src, count, vals, feats, recv, peers):
    width, nodes = feats.shape
    own = nodes // edge
    domains = recv.shape[0]
    return pl.pallas_call(
        gather_kernel,
        out_shape=jax.ShapeDtypeStruct((peers, width, nodes // peers), bf16),
        in_specs=[hbm] * 5 + [vmem],
        out_specs=vmem,
        scratch_shapes=[
            pltpu.VMEM((width, nodes), bf16),
            pltpu.VMEM((own + domains // 2 + domains, width, edge), bf16),
            pltpu.VMEM((own + 1, width, edge), f32),
            pltpu.SemaphoreType.DMA,
        ]
        + tile_scratch(vals.shape[0]),
        compiler_params=params(32),
        name="gather",
    )(*far_off(dst, src), count, *far_off(vals, feats), recv)


def spread_kernel(
    dst_ref, src_ref, count_ref, vals_ref, near_ref, out_ref, base_ref, blocks, total, *scratch
):
    peers, width, _ = near_ref.shape
    own = blocks.shape[0]
    per = own // peers
    share = per * edge
    domains = out_ref.shape[0]
    far = own + domains // 2

    def summed(place):
        start = share + place * edge
        return jnp.sum(near_ref[:, :, start : start + edge].astype(f32), axis=0)

    def prepare():
        for b in range(own):
            col = (b % per) * edge
            blocks[b] = near_ref[b // per, :, col : col + edge]
        total[...] = jnp.zeros_like(total)

    walk_tiles((dst_ref, src_ref, count_ref, vals_ref), scratch, prepare, blocks, total, False)
    grad_self = summed(0).astype(bf16)
    grad_neigh = summed(1).astype(bf16)
    grad_bias = column_block(jnp.sum(summed(2), axis=1, keepdims=True))
    grad_bias = pltpu.roll(grad_bias, edge // 2, 1)
    lane = lanes(width)
    for g in range(domains // 2):
        here = total[own + g]
        for odd in range(2):
            q = 2 * g + odd
            mine = pltpu.roll(here, edge // 2, 1) if odd else here
            out_ref[q, 0:width] = total[far + q].astype(bf16)
            out_ref[q, width : 2 * width] = jnp.where(lane < edge // 2, mine, grad_bias).astype(bf16)
            out_ref[q, 2 * width : 3 * width] = grad_self
            out_ref[q, 3 * width : 4 * width] = grad_neigh
    for b in range(own):
        base_ref[:, b * edge : (b + 1) * edge] = total[b]


def spread(dst, src, count, vals, near, domains, nodes):
    _, width, _ = near.shape
    own = nodes // edge
    return pl.pallas_call(
        spread_kernel,
        out_shape=(
            jax.ShapeDtypeStruct((domains, 4 * width, edge), bf16),
            jax.ShapeDtypeStruct((width, nodes), f32),
        ),
        in_specs=[hbm] * 4 + [vmem],
        out_specs=(vmem, vmem),
        scratch_shapes=[
            pltpu.VMEM((own, width, edge), bf16),
            pltpu.VMEM((own + domains // 2 + domains + 1, width, edge), f32),
        ]
        + tile_scratch(vals.shape[0]),
        compiler_params=params(32),
        name="spread",
    )(*far_off(dst, src), count, *far_off(vals), near)


def hot_kernel(index, hots):
    sub = lax.broadcasted_iota(jnp.int32, (span, edge), 0)
    groups = index.shape[0]
    for g in range(groups):
        hot = jnp.where(sub == (index[g : g + 1, :] & (span - 1)), 1.0, 0.0).astype(bf16)
        hots[:, g * edge : (g + 1) * edge] = hot
    for g in range(groups, groups + 2):
        hots[:, g * edge : (g + 1) * edge] = hot


def hot_columns(index):
    return pl.pallas_call(
        hot_kernel,
        out_shape=jax.ShapeDtypeStruct((span, (index.shape[0] + 2) * edge), bf16),
        in_specs=[vmem],
        out_specs=vmem,
        compiler_params=params(16),
        name="hot_columns",
    )(index)


def layer_kernel(agg_ref, *rest):
    peers, width, share = agg_ref.shape
    rows = peers * width
    parts, near_ref, lates = rest[:peers], rest[peers], rest[peers + 1 : 2 * peers + 1]
    feats_all, cotangent_all, self_all, neigh_all, bias_all, act, back = rest[2 * peers + 1 :]
    here = lax.axis_index("feat")
    for k, part in enumerate(parts):
        peer = here ^ k
        feats_all[peer] = part[:, 0:share]
        cotangent_all[peer] = part[:, share : 2 * share]
        self_all[peer] = part[:, 2 * share : 2 * share + edge]
        neigh_all[peer] = part[:, 2 * share + edge : 2 * share + 2 * edge]
        bias_all[peer] = part[:, 2 * share + 2 * edge : 2 * share + 3 * edge]
    feats = feats_all[...].reshape(rows, share)
    cotangent = cotangent_all[...].reshape(rows, share)
    w_self = self_all[...].reshape(rows, edge)
    w_neigh = neigh_all[...].reshape(rows, edge)
    bias = jnp.sum(bias_all[...].reshape(rows, edge).astype(f32), axis=1, keepdims=True)
    aggregate = agg_ref[...].reshape(rows, share)
    first = (((0,), (0,)), ((), ()))
    last = (((1,), (1,)), ((), ()))
    linear = lax.dot_general(w_self, feats, first, preferred_element_type=f32)
    linear = linear + lax.dot_general(w_neigh, aggregate, first, preferred_element_type=f32)
    linear = linear + bias
    logistic = jax.nn.sigmoid(linear)
    act[...] = (linear * logistic).astype(bf16).reshape(peers, width, share)
    slope = logistic * (1.0 + linear * (1.0 - logistic))
    grad = (cotangent.astype(f32) * slope).astype(bf16)
    near_ref[:, :, 0:share] = (
        jnp.dot(w_neigh, grad, preferred_element_type=f32).astype(bf16).reshape(peers, width, share)
    )
    back[...] = (
        jnp.dot(w_self, grad, preferred_element_type=f32).astype(bf16).reshape(peers, width, share)
    )
    grad_self = lax.dot_general(feats, grad, last, preferred_element_type=f32)
    grad_neigh = lax.dot_general(aggregate, grad, last, preferred_element_type=f32)
    grad_bias = column_block(jnp.sum(grad.astype(f32), axis=1, keepdims=True)).astype(bf16)
    for place, piece in enumerate((grad_self.astype(bf16), grad_neigh.astype(bf16), grad_bias)):
        start = share + place * edge
        near_ref[:, :, start : start + edge] = piece.reshape(peers, width, edge)
    for k, late in enumerate(lates):
        peer = here ^ k
        late[:, 0:share] = act[peer]
        late[:, share : 2 * share] = back[peer]


def layer(agg, parts):
    peers, width, share = agg.shape
    return pl.pallas_call(
        layer_kernel,
        out_shape=(jax.ShapeDtypeStruct((peers, width, share + 3 * edge), bf16),)
        + (jax.ShapeDtypeStruct((width, 2 * share), bf16),) * peers,
        in_specs=[vmem] * (1 + peers),
        out_specs=(vmem,) * (1 + peers),
        scratch_shapes=[
            pltpu.VMEM((peers, width, share), bf16),
            pltpu.VMEM((peers, width, share), bf16),
            pltpu.VMEM((peers, width, edge), bf16),
            pltpu.VMEM((peers, width, edge), bf16),
            pltpu.VMEM((peers, width, edge), bf16),
            pltpu.VMEM((peers, width, share), bf16),
            pltpu.VMEM((peers, width, share), bf16),
        ],
        compiler_params=params(32),
        name="layer",
    )(agg, *parts)


def settle_kernel(scale, index, hots, recv_ref, base_ref, *rest):
    width, nodes = base_ref.shape
    lates, rest = rest[:-7], rest[-7:]
    act_ref, feats_ref, self_ref, neigh_ref, bias_ref, marked, back = rest
    domains = recv_ref.shape[0]
    peers = len(lates)
    share = nodes // peers
    count = nodes // span
    pairs = domains // 2
    here = lax.axis_index("feat")
    for k, late in enumerate(lates):
        peer = here ^ k
        act_ref[:, pl.ds(pl.multiple_of(peer * share, share), share)] = late[:, 0:share]
        back[:, pl.ds(pl.multiple_of(peer * share, share), share)] = late[:, share : 2 * share]
    lane = lanes(width)

    def over(start):
        return jnp.sum(recv_ref[:, start : start + width].astype(f32), axis=0)

    hub = over(0)
    self_ref[...] = over(2 * width) * scale
    neigh_ref[...] = over(3 * width) * scale
    tail = jnp.where(lane >= edge // 2, over(width), 0.0)
    column = jnp.broadcast_to(jnp.sum(tail, axis=1, keepdims=True) * scale, (width, edge))
    row = lax.broadcasted_iota(jnp.int32, (width, edge), 0)
    bias_ref[...] = jnp.sum(jnp.where(row == lane, column, 0.0), axis=0)[:width]
    hub_pieces = split(hub, 3)
    for g in range(pairs + 3):
        if g < pairs:
            first = recv_ref[2 * g, width : 2 * width].astype(f32)
            second = pltpu.roll(recv_ref[2 * g + 1, width : 2 * width].astype(f32), edge // 2, 1)
            value = jnp.where(lane < edge // 2, first, second)
        else:
            value = hub_pieces[g - pairs].astype(f32)
        at = min(g, pairs)
        where = jnp.broadcast_to(index[at : at + 1, :] >> 8, (width, edge))
        for b in range(count):
            marked[b * width : (b + 1) * width, g * edge : (g + 1) * edge] = jnp.where(
                where == b, value, 0.0
            ).astype(bf16)
    placed = lax.dot_general(
        marked[...], hots[...], (((1,), (1,)), ((), ())), preferred_element_type=f32
    )
    for b in range(count):
        cols = slice(b * span, (b + 1) * span)
        feats_ref[:, cols] = (
            back[:, cols].astype(f32) + base_ref[:, cols] + placed[b * width : (b + 1) * width]
        ).astype(bf16)


def settle(index, hots, recv, base, lates, scale):
    width, nodes = base.shape
    domains = recv.shape[0]
    terms = (domains // 2 + 3) * edge
    return pl.pallas_call(
        functools.partial(settle_kernel, scale),
        out_shape=(
            jax.ShapeDtypeStruct((width, nodes), bf16),
            jax.ShapeDtypeStruct((width, nodes), bf16),
            jax.ShapeDtypeStruct((width, edge), f32),
            jax.ShapeDtypeStruct((width, edge), f32),
            jax.ShapeDtypeStruct((width,), f32),
        ),
        in_specs=[vmem] * (4 + len(lates)),
        out_specs=(vmem,) * 5,
        scratch_shapes=[
            pltpu.VMEM((nodes // span * width, terms), bf16),
            pltpu.VMEM((width, nodes), bf16),
        ],
        compiler_params=params(32),
        name="settle",
    )(index, hots, recv, base, *lates)


def swap(values, axis):
    return lax.all_to_all(values, axis, split_axis=0, concat_axis=0, tiled=True)


def trade(parts, axis):
    peers = len(parts)
    return [
        part if k == 0 else lax.ppermute(part, axis, [(i, i ^ k) for i in range(peers)])
        for k, part in enumerate(parts)
    ]


def local(
    feats,
    tile_vals,
    tile_dst,
    tile_src,
    tile_count,
    send_rows,
    hub_ids,
    w_self,
    w_neigh,
    bias,
    cotangent,
):
    nodes = feats.shape[1]
    domains = lax.axis_size("dom")
    peers = lax.axis_size("feat")
    picked, index, *parts = pick(
        send_rows[0],
        hub_ids,
        feats,
        cotangent,
        w_self,
        w_neigh,
        bias,
        peers,
    )
    recv = swap(picked, "dom")
    parts = trade(parts, "feat")
    agg = gather(tile_dst, tile_src, tile_count, tile_vals, feats, recv, peers)
    agg, parts = lax.optimization_barrier((agg, parts))
    agg = swap(agg, "feat")
    near, *lates = layer(agg, parts)
    near = swap(near, "feat")
    back, base = spread(tile_dst, tile_src, tile_count, tile_vals, near, domains, nodes)
    back, lates, index = lax.optimization_barrier((back, lates, index))
    back = swap(back, "dom")
    lates = trade(lates, "feat")
    hots = hot_columns(index)
    scale = 1.0 / math.sqrt(nodes * domains)
    return settle(index, hots, back, base, lates, scale)


def solution(mesh):
    placed = (
        P("feat", "dom"),
        P("dom", None, None),
        P("dom"),
        P("dom"),
        P("dom"),
        P("dom", None, None),
        P("dom"),
        P("feat", None),
        P("feat", None),
        P("feat"),
        P("feat", "dom"),
    )
    return jax.shard_map(
        local,
        mesh=mesh,
        in_specs=placed,
        out_specs=(P("feat", "dom"), P("feat", "dom"), P("feat", None), P("feat", None), P("feat")),
        check_vma=False,
    )
```

```python
import functools
import math

import jax
import jax.numpy as jnp
from jax import lax
from jax.experimental import pallas as pl
from jax.experimental.pallas import tpu as pltpu
from jax.sharding import PartitionSpec as P

edge = 128
span = 256
group = 64
sure = 1
bf16 = jnp.bfloat16
f32 = jnp.float32
vmem = pl.BlockSpec(memory_space=pltpu.VMEM)
smem = pl.BlockSpec(memory_space=pltpu.SMEM)
hbm = pl.BlockSpec(memory_space=pl.ANY)


def params(mib):
    return pltpu.CompilerParams(vmem_limit_bytes=mib * 1024 * 1024)


def far_off(*values):
    return [pltpu.with_memory_space_constraint(value, pltpu.HBM) for value in values]


def lanes(rows):
    return lax.broadcasted_iota(jnp.int32, (rows, edge), 1)


def split(values, pieces):
    parts = []
    for _ in range(pieces):
        part = values.astype(bf16)
        parts.append(part)
        values = values - part.astype(f32)
    return parts


def column_block(column):
    hi, mid, lo = split(column, 3)
    lane = lanes(column.shape[0])
    block = jnp.where(lane == 0, hi.astype(f32), 0.0)
    block = jnp.where(lane == 1, mid.astype(f32), block)
    return jnp.where(lane == 2, lo.astype(f32), block)


def ways(peers):
    return sorted(range(peers), key=lambda k: -k.bit_length())


def start_all(pairs, sems):
    copies = []
    for place, (source, target) in enumerate(pairs):
        copies.append(pltpu.make_async_copy(source, target, sems.at[place]))
        copies[-1].start()
    return copies


def pick_kernel(
    rows_ref,
    hub_ref,
    feats_ref,
    cotangent_ref,
    self_ref,
    neigh_ref,
    bias_ref,
    out_ref,
    index,
    *rest,
):
    parts, rest = rest[:-10], rest[-10:]
    near, hub, wide, blocks, picked, w_self, w_neigh, bias, sems, part_sems = rest
    width, nodes = feats_ref.shape
    span_count = nodes // span
    pairs = rows_ref.shape[0] // 2
    peers = len(parts)
    share = nodes // peers
    half = edge // 2
    copies = start_all(
        (
            (rows_ref, wide),
            (hub_ref, hub),
            (feats_ref, near),
            (self_ref, w_self),
            (neigh_ref, w_neigh),
            (bias_ref, bias),
        ),
        sems,
    )
    here = lax.axis_index("feat")
    moves = []
    for k, part in zip(ways(peers), parts):
        there = pl.ds(pl.multiple_of((here ^ k) * share, share), share)
        moves.append((feats_ref.at[:, there], part.at[:, 0:share]))
        moves.append((cotangent_ref.at[:, there], part.at[:, share : 2 * share]))
    moves = start_all(moves, part_sems)
    for copy in copies[:2]:
        copy.wait()
    for g in range(pairs):
        row = jnp.concatenate([wide[2 * g : 2 * g + 1, :], wide[2 * g + 1 : 2 * g + 2, :]], axis=1)
        index[g : g + 1, :] = row
    index[pairs : pairs + 1, :] = hub[...].reshape(1, edge)
    for copy in copies[2:]:
        copy.wait()
    for b in range(span_count):
        blocks[b] = near[:, b * span : (b + 1) * span]
    sub = lax.broadcasted_iota(jnp.int32, (span, edge), 0)

    def find(g, carry):
        row = index[pl.ds(g, 1), :]
        home = jnp.broadcast_to(row >> 8, (width, edge))
        hot = jnp.where(sub == (row & (span - 1)), 1.0, 0.0).astype(bf16)
        whole = blocks[...].reshape(span_count * width, span)
        found = jnp.dot(whole, hot, preferred_element_type=f32)
        total = found[0:width]
        for b in range(1, span_count):
            total = jnp.where(home == b, found[b * width : (b + 1) * width], total)
        picked[g] = total
        return carry

    lax.fori_loop(0, pairs, find, 0, unroll=pairs)
    find(pairs, 0)
    lane = lanes(width)
    mine = picked[pairs].astype(bf16)
    for g in range(pairs):
        here = picked[g]
        turned = pltpu.roll(here, half, 1)
        for odd in range(2):
            first, second = (turned, here) if odd else (here, turned)
            out_ref[2 * g + odd, 0:width] = mine
            out_ref[2 * g + odd, width : 2 * width] = jnp.where(lane < half, first, second).astype(
                bf16
            )
    square = (width, width)
    diagonal = lax.broadcasted_iota(jnp.int32, square, 0) == lax.broadcasted_iota(
        jnp.int32, square, 1
    )
    spread_bias = jnp.broadcast_to(bias[...].reshape(1, width), square)
    column = jnp.sum(jnp.where(diagonal, spread_bias, 0.0), axis=1, keepdims=True)
    block = column_block(column).astype(bf16)
    for part in parts:
        part[:, 2 * share : 2 * share + edge] = w_self[...]
        part[:, 2 * share + edge : 2 * share + 2 * edge] = w_neigh[...]
        part[:, 2 * share + 2 * edge : 2 * share + 3 * edge] = block
    for move in moves:
        move.wait()


def pick(rows, hub_ids, feats, cotangent, w_self, w_neigh, bias, peers):
    width, nodes = feats.shape
    domains, slots = rows.shape
    groups = domains // 2 + 1
    part = jax.ShapeDtypeStruct((width, 2 * nodes // peers + 3 * edge), bf16)
    return pl.pallas_call(
        pick_kernel,
        out_shape=(
            jax.ShapeDtypeStruct((domains, 2 * width, edge), bf16),
            jax.ShapeDtypeStruct((groups, edge), jnp.int32),
        )
        + (part,) * peers,
        in_specs=[hbm] * 7,
        out_specs=(vmem,) * (2 + peers),
        scratch_shapes=[
            pltpu.VMEM((width, nodes), bf16),
            pltpu.VMEM((edge,), jnp.int32),
            pltpu.VMEM((domains, slots), jnp.int32),
            pltpu.VMEM((nodes // span, width, span), bf16),
            pltpu.VMEM((groups, width, edge), f32),
            pltpu.VMEM((width, edge), bf16),
            pltpu.VMEM((width, edge), bf16),
            pltpu.VMEM((width,), f32),
            pltpu.SemaphoreType.DMA((7,)),
            pltpu.SemaphoreType.DMA((2 * peers,)),
        ],
        compiler_params=params(32),
        name="pick",
    )(*far_off(rows, hub_ids, feats, cotangent, w_self, w_neigh, bias))


def products_of(lefts, tiles, turned):
    results = []
    for i in range(0, len(tiles), 2):
        left = jnp.concatenate([lefts[i], lefts[i + 1]], axis=0)
        right = jnp.concatenate([tiles[i], tiles[i + 1]], axis=0 if turned else 1)
        contract = (((1,), (1 if turned else 0,)), ((), ()))
        both = lax.dot_general(left, right, contract, preferred_element_type=f32)
        width = lefts[i].shape[0]
        results += [both[:width, :edge], both[width:, edge:]]
    return results


def walk_tiles(refs, scratch, prepare, table, total, turned):
    dst_ref, src_ref, count_ref, vals_ref = refs
    dst, src, count, held, sems, tile_sems = scratch
    spare = total.shape[0] - 1
    lists = [
        pltpu.make_async_copy(count_ref, count, sems.at[0]),
        pltpu.make_async_copy(dst_ref, dst, sems.at[1]),
        pltpu.make_async_copy(src_ref, src, sems.at[2]),
    ]

    def fetch(k):
        rows = pl.ds(k * group, group)
        return pltpu.make_async_copy(vals_ref.at[rows], held.at[rows], tile_sems.at[k])

    def begin(k, carry):
        fetch(k).start()
        return carry

    for copy in lists:
        copy.start()
    for k in range(sure):
        fetch(k).start()
    prepare()
    lists[0].wait()
    live = count[0]
    groups = (live + group - 1) // group
    lax.fori_loop(sure, groups, begin, 0)
    for copy in lists[1:]:
        copy.wait()

    def some(k, carry):
        first = k * group
        lefts, places = [], []
        for i in range(group):
            t = first + i
            target, source = dst[t], src[t]
            lefts.append(table[source if turned else target])
            places.append(jnp.where(t < live, target if turned else source, spare))
        fetch(k).wait()
        tiles = [held[first + i] for i in range(group)]
        for place, product in zip(places, products_of(lefts, tiles, turned)):
            total[place] += product
        return carry

    lax.fori_loop(0, groups, some, 0)


def tile_scratch(tiles):
    return [
        pltpu.SMEM((tiles,), jnp.int32),
        pltpu.SMEM((tiles,), jnp.int32),
        pltpu.SMEM((1,), jnp.int32),
        pltpu.VMEM((tiles, edge, edge), bf16),
        pltpu.SemaphoreType.DMA((3,)),
        pltpu.SemaphoreType.DMA((tiles // group,)),
    ]


def gather_kernel(
    dst_ref, src_ref, count_ref, vals_ref, feats_ref, recv_ref, out_ref, near, table, total, sem, *scratch
):
    width, nodes = feats_ref.shape
    own = nodes // edge
    domains = recv_ref.shape[0]
    peers = out_ref.shape[0]
    features = pltpu.make_async_copy(feats_ref, near, sem)
    features.start()

    def prepare():
        lane = lanes(width)
        for g in range(domains // 2):
            table[own + g] = jnp.where(
                lane < edge // 2,
                recv_ref[2 * g, width : 2 * width].astype(f32),
                recv_ref[2 * g + 1, width : 2 * width].astype(f32),
            ).astype(bf16)
        for q in range(domains):
            table[own + domains // 2 + q] = recv_ref[q, 0:width]
        total[...] = jnp.zeros_like(total)
        features.wait()
        for b in range(own):
            table[b] = near[:, b * edge : (b + 1) * edge]

    walk_tiles((dst_ref, src_ref, count_ref, vals_ref), scratch, prepare, table, total, True)
    per = own // peers
    for b in range(own):
        col = (b % per) * edge
        out_ref[b // per, :, col : col + edge] = total[b].astype(bf16)


def gather(dst, src, count, vals, feats, recv, peers):
    width, nodes = feats.shape
    own = nodes // edge
    domains = recv.shape[0]
    return pl.pallas_call(
        gather_kernel,
        out_shape=jax.ShapeDtypeStruct((peers, width, nodes // peers), bf16),
        in_specs=[hbm] * 5 + [vmem],
        out_specs=vmem,
        scratch_shapes=[
            pltpu.VMEM((width, nodes), bf16),
            pltpu.VMEM((own + domains // 2 + domains, width, edge), bf16),
            pltpu.VMEM((own + 1, width, edge), f32),
            pltpu.SemaphoreType.DMA,
        ]
        + tile_scratch(vals.shape[0]),
        compiler_params=params(32),
        name="gather",
    )(*far_off(dst, src), count, *far_off(vals, feats), recv)


def spread_kernel(
    dst_ref, src_ref, count_ref, vals_ref, near_ref, out_ref, base_ref, blocks, total, tail, *scratch
):
    peers, width, _ = near_ref.shape
    own = blocks.shape[0]
    per = own // peers
    share = per * edge
    domains = out_ref.shape[0]
    far = own + domains // 2

    def summed(place):
        start = share + place * edge
        return jnp.sum(near_ref[:, :, start : start + edge].astype(f32), axis=0)

    def prepare():
        for b in range(own):
            col = (b % per) * edge
            blocks[b] = near_ref[b // per, :, col : col + edge]
        total[...] = jnp.zeros_like(total)
        grad_self = summed(0).astype(bf16)
        grad_neigh = summed(1).astype(bf16)
        grad_bias = column_block(jnp.sum(summed(2), axis=1, keepdims=True))
        tail[...] = pltpu.roll(grad_bias, edge // 2, 1)
        for q in range(domains):
            out_ref[q, 2 * width : 3 * width] = grad_self
            out_ref[q, 3 * width : 4 * width] = grad_neigh

    walk_tiles((dst_ref, src_ref, count_ref, vals_ref), scratch, prepare, blocks, total, False)
    grad_bias = tail[...]
    lane = lanes(width)
    for g in range(domains // 2):
        here = total[own + g]
        for odd in range(2):
            q = 2 * g + odd
            mine = pltpu.roll(here, edge // 2, 1) if odd else here
            out_ref[q, 0:width] = total[far + q].astype(bf16)
            out_ref[q, width : 2 * width] = jnp.where(lane < edge // 2, mine, grad_bias).astype(bf16)
    for b in range(own):
        base_ref[:, b * edge : (b + 1) * edge] = total[b]


def spread(dst, src, count, vals, near, domains, nodes):
    _, width, _ = near.shape
    own = nodes // edge
    return pl.pallas_call(
        spread_kernel,
        out_shape=(
            jax.ShapeDtypeStruct((domains, 4 * width, edge), bf16),
            jax.ShapeDtypeStruct((width, nodes), f32),
        ),
        in_specs=[hbm] * 4 + [vmem],
        out_specs=(vmem, vmem),
        scratch_shapes=[
            pltpu.VMEM((own, width, edge), bf16),
            pltpu.VMEM((own + domains // 2 + domains + 1, width, edge), f32),
            pltpu.VMEM((width, edge), f32),
        ]
        + tile_scratch(vals.shape[0]),
        compiler_params=params(32),
        name="spread",
    )(*far_off(dst, src), count, *far_off(vals), near)


def hot_kernel(index, hots):
    sub = lax.broadcasted_iota(jnp.int32, (span, edge), 0)
    groups = index.shape[0]
    for g in range(groups):
        hot = jnp.where(sub == (index[g : g + 1, :] & (span - 1)), 1.0, 0.0).astype(bf16)
        hots[:, g * edge : (g + 1) * edge] = hot
    for g in range(groups, groups + 2):
        hots[:, g * edge : (g + 1) * edge] = hot


def hot_columns(index):
    return pl.pallas_call(
        hot_kernel,
        out_shape=jax.ShapeDtypeStruct((span, (index.shape[0] + 2) * edge), bf16),
        in_specs=[vmem],
        out_specs=vmem,
        compiler_params=params(16),
        name="hot_columns",
    )(index)


def layer_kernel(agg_ref, *rest):
    peers, width, share = agg_ref.shape
    rows = peers * width
    parts, near_ref, lates = rest[:peers], rest[peers], rest[peers + 1 : 2 * peers + 1]
    feats_all, cotangent_all, self_all, neigh_all, bias_all, act, back = rest[2 * peers + 1 :]
    here = lax.axis_index("feat")
    for k, part in zip(ways(peers), parts):
        peer = here ^ k
        feats_all[peer] = part[:, 0:share]
        cotangent_all[peer] = part[:, share : 2 * share]
        self_all[peer] = part[:, 2 * share : 2 * share + edge]
        neigh_all[peer] = part[:, 2 * share + edge : 2 * share + 2 * edge]
        bias_all[peer] = part[:, 2 * share + 2 * edge : 2 * share + 3 * edge]
    feats = feats_all[...].reshape(rows, share)
    cotangent = cotangent_all[...].reshape(rows, share)
    w_self = self_all[...].reshape(rows, edge)
    w_neigh = neigh_all[...].reshape(rows, edge)
    bias = jnp.sum(bias_all[...].reshape(rows, edge).astype(f32), axis=1, keepdims=True)
    aggregate = agg_ref[...].reshape(rows, share)
    first = (((0,), (0,)), ((), ()))
    last = (((1,), (1,)), ((), ()))
    linear = lax.dot_general(w_self, feats, first, preferred_element_type=f32)
    linear = linear + lax.dot_general(w_neigh, aggregate, first, preferred_element_type=f32)
    linear = linear + bias
    logistic = jax.nn.sigmoid(linear)
    act[...] = (linear * logistic).astype(bf16).reshape(peers, width, share)
    slope = logistic * (1.0 + linear * (1.0 - logistic))
    grad = (cotangent.astype(f32) * slope).astype(bf16)
    near_ref[:, :, 0:share] = (
        jnp.dot(w_neigh, grad, preferred_element_type=f32).astype(bf16).reshape(peers, width, share)
    )
    back[...] = (
        jnp.dot(w_self, grad, preferred_element_type=f32).astype(bf16).reshape(peers, width, share)
    )
    grad_self = lax.dot_general(feats, grad, last, preferred_element_type=f32)
    grad_neigh = lax.dot_general(aggregate, grad, last, preferred_element_type=f32)
    grad_bias = column_block(jnp.sum(grad.astype(f32), axis=1, keepdims=True)).astype(bf16)
    for place, piece in enumerate((grad_self.astype(bf16), grad_neigh.astype(bf16), grad_bias)):
        start = share + place * edge
        near_ref[:, :, start : start + edge] = piece.reshape(peers, width, edge)
    for k, late in zip(ways(peers), lates):
        peer = here ^ k
        late[:, 0:share] = act[peer]
        late[:, share : 2 * share] = back[peer]


def layer(agg, parts):
    peers, width, share = agg.shape
    return pl.pallas_call(
        layer_kernel,
        out_shape=(jax.ShapeDtypeStruct((peers, width, share + 3 * edge), bf16),)
        + (jax.ShapeDtypeStruct((width, 2 * share), bf16),) * peers,
        in_specs=[vmem] * (1 + peers),
        out_specs=(vmem,) * (1 + peers),
        scratch_shapes=[
            pltpu.VMEM((peers, width, share), bf16),
            pltpu.VMEM((peers, width, share), bf16),
            pltpu.VMEM((peers, width, edge), bf16),
            pltpu.VMEM((peers, width, edge), bf16),
            pltpu.VMEM((peers, width, edge), bf16),
            pltpu.VMEM((peers, width, share), bf16),
            pltpu.VMEM((peers, width, share), bf16),
        ],
        compiler_params=params(32),
        name="layer",
    )(agg, *parts)


def settle_kernel(scale, index, hots, recv_ref, base_ref, *rest):
    width, nodes = base_ref.shape
    lates, rest = rest[:-7], rest[-7:]
    act_ref, feats_ref, self_ref, neigh_ref, bias_ref, marked, back = rest
    domains = recv_ref.shape[0]
    peers = len(lates)
    share = nodes // peers
    count = nodes // span
    pairs = domains // 2
    here = lax.axis_index("feat")
    for k, late in zip(ways(peers), lates):
        peer = here ^ k
        act_ref[:, pl.ds(pl.multiple_of(peer * share, share), share)] = late[:, 0:share]
        back[:, pl.ds(pl.multiple_of(peer * share, share), share)] = late[:, share : 2 * share]
    lane = lanes(width)

    def over(start):
        return jnp.sum(recv_ref[:, start : start + width].astype(f32), axis=0)

    hub = over(0)
    self_ref[...] = over(2 * width) * scale
    neigh_ref[...] = over(3 * width) * scale
    tail = jnp.where(lane >= edge // 2, over(width), 0.0)
    column = jnp.broadcast_to(jnp.sum(tail, axis=1, keepdims=True) * scale, (width, edge))
    row = lax.broadcasted_iota(jnp.int32, (width, edge), 0)
    bias_ref[...] = jnp.sum(jnp.where(row == lane, column, 0.0), axis=0)[:width]
    hub_pieces = split(hub, 3)
    for g in range(pairs + 3):
        if g < pairs:
            first = recv_ref[2 * g, width : 2 * width].astype(f32)
            second = pltpu.roll(recv_ref[2 * g + 1, width : 2 * width].astype(f32), edge // 2, 1)
            value = jnp.where(lane < edge // 2, first, second)
        else:
            value = hub_pieces[g - pairs].astype(f32)
        at = min(g, pairs)
        where = jnp.broadcast_to(index[at : at + 1, :] >> 8, (width, edge))
        for b in range(count):
            marked[b * width : (b + 1) * width, g * edge : (g + 1) * edge] = jnp.where(
                where == b, value, 0.0
            ).astype(bf16)
    placed = lax.dot_general(
        marked[...], hots[...], (((1,), (1,)), ((), ())), preferred_element_type=f32
    )
    for b in range(count):
        cols = slice(b * span, (b + 1) * span)
        feats_ref[:, cols] = (
            back[:, cols].astype(f32) + base_ref[:, cols] + placed[b * width : (b + 1) * width]
        ).astype(bf16)


def settle(index, hots, recv, base, lates, scale):
    width, nodes = base.shape
    domains = recv.shape[0]
    terms = (domains // 2 + 3) * edge
    return pl.pallas_call(
        functools.partial(settle_kernel, scale),
        out_shape=(
            jax.ShapeDtypeStruct((width, nodes), bf16),
            jax.ShapeDtypeStruct((width, nodes), bf16),
            jax.ShapeDtypeStruct((width, edge), f32),
            jax.ShapeDtypeStruct((width, edge), f32),
            jax.ShapeDtypeStruct((width,), f32),
        ),
        in_specs=[vmem] * (4 + len(lates)),
        out_specs=(vmem,) * 5,
        scratch_shapes=[
            pltpu.VMEM((nodes // span * width, terms), bf16),
            pltpu.VMEM((width, nodes), bf16),
        ],
        compiler_params=params(32),
        name="settle",
    )(index, hots, recv, base, *lates)


def swap(values, axis):
    return lax.all_to_all(values, axis, split_axis=0, concat_axis=0, tiled=True)


def trade(parts, axis):
    peers = len(parts)
    return [
        lax.ppermute(part, axis, [(i, i ^ k) for i in range(peers)]) if k else part
        for k, part in zip(ways(peers), parts)
    ]


def local(
    feats,
    tile_vals,
    tile_dst,
    tile_src,
    tile_count,
    send_rows,
    hub_ids,
    w_self,
    w_neigh,
    bias,
    cotangent,
):
    nodes = feats.shape[1]
    domains = lax.axis_size("dom")
    peers = lax.axis_size("feat")
    picked, index, *parts = pick(
        send_rows[0],
        hub_ids,
        feats,
        cotangent,
        w_self,
        w_neigh,
        bias,
        peers,
    )
    recv = swap(picked, "dom")
    parts = trade(parts, "feat")
    agg = gather(tile_dst, tile_src, tile_count, tile_vals, feats, recv, peers)
    agg, parts = lax.optimization_barrier((agg, parts))
    agg = swap(agg, "feat")
    near, *lates = layer(agg, parts)
    near = swap(near, "feat")
    back, base = spread(tile_dst, tile_src, tile_count, tile_vals, near, domains, nodes)
    back, lates, index = lax.optimization_barrier((back, lates, index))
    back = swap(back, "dom")
    lates = trade(lates, "feat")
    hots = hot_columns(index)
    scale = 1.0 / math.sqrt(nodes * domains)
    return settle(index, hots, back, base, lates, scale)


def solution(mesh):
    placed = (
        P("feat", "dom"),
        P("dom", None, None),
        P("dom"),
        P("dom"),
        P("dom"),
        P("dom", None, None),
        P("dom"),
        P("feat", None),
        P("feat", None),
        P("feat"),
        P("feat", "dom"),
    )
    return jax.shard_map(
        local,
        mesh=mesh,
        in_specs=placed,
        out_specs=(P("feat", "dom"), P("feat", "dom"), P("feat", None), P("feat", None), P("feat")),
        check_vma=False,
    )
```
